256 devices in a mesh: dp: 8 (over y, core), seq: 32 (over x, z).
Axes of the slice: x: 4, y: 4, z: 8, core: 2. Of those that a mesh axis runs over, the one named last changes fastest.
Arguments:
- query_in: bfloat16 [8, 4096, 2048], P('dp', 'seq'), may hold values from -5.5 to 5.5
- key_in: bfloat16 [8, 4096, 2048], P('dp', 'seq'), may hold values from -5.5 to 5.5
- value_in: bfloat16 [8, 4096, 2048], P('dp', 'seq'), may hold values from -6 to 6
- residual: bfloat16 [8, 4096, 3072], P(None, 'seq', 'dp'), may hold values from -6 to 6
- out_proj: bfloat16 [2048, 3072], P(None, 'dp'), may hold values from -2 to 2
- first_proj: bfloat16 [3072, 2048], P('dp'), may hold values from -0.109375 to 0.109375
- first_bias: float32 [2048], replicated, may hold values from -3 to 3
- second_proj: bfloat16 [2048, 1536], P('dp'), may hold values from -0.125 to 0.125
- second_bias: float32 [1536], replicated, may hold values from -3 to 3
- teacher: bfloat16 [8, 512, 1536], P('dp', 'seq'), may hold values from -6 to 6
- teach_index: int32 [4096, 4], P('seq'), may hold values from 0 to 511, as said below
- teach_weight: float32 [4096, 4], P('seq'), may hold values from 0.2 to 2
Outputs:
- similarity: float32 [8, 4096], P('dp', 'seq')
- grad_first: bfloat16 [3072, 2048], P('dp')
- grad_second: bfloat16 [2048, 1536], P('dp')
The draws below stay inside these ranges and needn't reach their ends.
Inputs may be any that keep to these rules, and one draw needn't show every extreme that they name: `teach_index`: each row named for a token held by seq index s belongs to the teacher rows held by seq indices s - 1, s or s + 1.
All inputs are finite; a program needn't handle non-finite values.
Results may differ from the reference program's by a relative error of at most 0.03.
Values may be sent and summed in bfloat16 or wider, within the bound.
No kernel may reach another device: no remote copies, remote signals or barrier semaphores. Data moves between devices by JAX's collectives and lax.ppermute only.
A program may use at most 64 MiB of HBM per device.

```python
import math
import jax
import jax.numpy as jnp
from jax import lax

D = 3072
HEAD_DIM = 64
HID = 2048
OUTF = 1536
TAPS = 4
TOK_DEV = 128
HEADS = 32
INNER = 2048
CLIPS = 8
LENGTH = 4096
TEACH_DEV = 16
TEACH = 512
N_DP = 8


def draw_query_in(key, part):
    key = jax.random.fold_in(key, 11)
    values = jnp.clip(jax.random.normal(key, (CLIPS, LENGTH, INNER), jnp.float32), -5.5, 5.5)
    return values.astype(jnp.bfloat16)


def draw_key_in(key, part):
    key = jax.random.fold_in(key, 12)
    values = jnp.clip(jax.random.normal(key, (CLIPS, LENGTH, INNER), jnp.float32), -5.5, 5.5)
    return values.astype(jnp.bfloat16)


def draw_teach_index(key, part):
    key = jax.random.fold_in(key, 3)
    token = jnp.arange(LENGTH, dtype=jnp.int32)
    base_row = token * TEACH_DEV // TOK_DEV
    offset = jax.random.randint(key, (LENGTH, TAPS), -TEACH_DEV, TEACH_DEV + 1)
    index = jnp.clip(base_row[:, None] + offset, 0, TEACH - 1)
    index = index.at[0, 0].set(0).at[LENGTH - 1, 0].set(TEACH - 1)
    return index.astype(jnp.int32)


def levels(own_key, extent, shards, least, largest):
    loudness = 1.0
    for position, shards_of in shards:
        draws = jax.random.uniform(jax.random.fold_in(jax.random.fold_in(own_key, 6), position), (shards_of,), jnp.float32, least / len(shards), largest / len(shards))
        loudness = loudness * jnp.repeat(jnp.exp(draws), extent[position] // shards_of).reshape((-1,) + (1,) * (len(extent) - 1 - position))
    return loudness


def gaussian(rng, dims, scale, bound, pieces=(), kind=jnp.bfloat16):
    values = scale * jax.random.normal(rng, dims, jnp.float32)
    if pieces:
        values = values * levels(rng, dims, pieces, -0.22, 0.18)
    return jnp.clip(values, -bound, bound).astype(kind)


def setup_inputs(seed: int = 0) -> dict:
    key_list = jax.random.split(jax.random.key(seed), 13)
    return {
        "query_in": draw_query_in(jax.random.fold_in(key_list[12], 71), 0),
        "key_in": draw_key_in(jax.random.fold_in(key_list[12], 71), 0),
        "value_in": gaussian(key_list[2], (CLIPS, LENGTH, INNER), 1.0, 6.0, ((0, 8), (1, 32))),
        "residual": gaussian(key_list[3], (CLIPS, LENGTH, D), 1.0, 6.0, ((1, 32), (2, 8))),
        "out_proj": gaussian(key_list[4], (INNER, D), (INNER // 256) ** -0.5, 2.0, ((1, 8),)),
        "first_proj": gaussian(key_list[5], (D, HID), D ** -0.5, 0.109375, ((0, 8),)),
        "first_bias": gaussian(key_list[6], (HID,), 0.5, 3.0, (), jnp.float32),
        "second_proj": gaussian(key_list[7], (HID, OUTF), HID ** -0.5, 0.125, ((0, 8),)),
        "second_bias": gaussian(key_list[8], (OUTF,), 0.5, 3.0, (), jnp.float32),
        "teacher": gaussian(key_list[9], (CLIPS, TEACH, OUTF), 1.0, 6.0, ((0, 8), (1, 32))),
        "teach_index": draw_teach_index(jax.random.fold_in(key_list[12], 71), 0),
        "teach_weight": jnp.clip(jnp.exp(math.log(2.0) - 2.3025851 * jax.random.uniform(key_list[11], (LENGTH, TAPS), jnp.float32) ** levels(key_list[11], (LENGTH, TAPS), ((0, 32),), -0.2, 0.2)), 0.2, 2.0),
    }


epsilon = 1e-06

def silu_slope(value):
    logistic = jax.nn.sigmoid(value)
    return logistic * (1.0 + value * (1.0 - logistic))

def round_partial(partial_value):
    return lax.optimization_barrier(partial_value.astype(jnp.bfloat16)).astype(jnp.float32)

def reference(query_in, key_in, value_in, residual, out_proj, first_proj, first_bias, second_proj, second_bias, teacher, teach_index, teach_weight):
    scale = HEAD_DIM ** (-0.5)
    block_rows = min(512, LENGTH)

    def one_head(triple):
        queries, keys_all, values_all = triple
        query_blocks = queries.reshape(LENGTH // block_rows, block_rows, HEAD_DIM)

        def one_block(query_block):
            scores = jnp.dot(query_block, keys_all.T, preferred_element_type=jnp.float32) * scale
            weights = jax.nn.softmax(scores, axis=-1).astype(jnp.bfloat16)
            return jnp.dot(weights, values_all, preferred_element_type=jnp.float32).astype(jnp.bfloat16)
        return lax.map(one_block, query_blocks).reshape(LENGTH, HEAD_DIM)

    def one_clip(triple):
        per_head = tuple((array.reshape(LENGTH, HEADS, HEAD_DIM).transpose(1, 0, 2) for array in triple))
        result = lax.map(one_head, per_head)
        return result.transpose(1, 0, 2).reshape(LENGTH, INNER)
    attended = lax.map(one_clip, (query_in, key_in, value_in))
    attn_rows = attended.reshape(-1, INNER)
    mixed = jnp.dot(attn_rows, out_proj, preferred_element_type=jnp.float32)
    hidden = (residual.reshape(-1, D) + mixed).astype(jnp.bfloat16)
    width_part = D // N_DP
    first_sum = jnp.zeros((hidden.shape[0], HID), jnp.float32)
    for shard in range(N_DP):
        low_edge = shard * width_part
        partial_value = jnp.dot(hidden[:, low_edge:low_edge + width_part], first_proj[low_edge:low_edge + width_part], preferred_element_type=jnp.float32)
        first_sum = first_sum + round_partial(partial_value)
    preact = first_sum + first_bias
    activated = jax.nn.silu(preact).astype(jnp.bfloat16)
    unit_part = HID // N_DP
    second_sum = jnp.zeros((hidden.shape[0], OUTF), jnp.float32)
    for shard in range(N_DP):
        low_edge = shard * unit_part
        partial_value = jnp.dot(activated[:, low_edge:low_edge + unit_part], second_proj[low_edge:low_edge + unit_part], preferred_element_type=jnp.float32)
        second_sum = second_sum + round_partial(partial_value)
    projected = second_sum + second_bias
    target = jnp.zeros((CLIPS, LENGTH, OUTF), jnp.float32)
    for tap_index in range(TAPS):
        picked = teacher[:, teach_index[:, tap_index], :].astype(jnp.float32)
        target = target + teach_weight[:, tap_index][None, :, None] * picked
    target = target.reshape(-1, OUTF)
    inv_model = lax.rsqrt(lax.optimization_barrier(jnp.sum(projected * projected, axis=1, keepdims=True)) + epsilon)
    inv_target = lax.rsqrt(lax.optimization_barrier(jnp.sum(target * target, axis=1, keepdims=True)) + epsilon)
    cosine = lax.optimization_barrier(jnp.sum(projected * target, axis=1, keepdims=True)) * inv_model * inv_target
    row_grad = (-math.sqrt(OUTF) * inv_model * (target * inv_target - cosine * inv_model * projected)).astype(jnp.bfloat16)
    second_grad = jnp.dot(activated.T, row_grad, preferred_element_type=jnp.float32)
    act_grad = jnp.dot(row_grad, second_proj.T, preferred_element_type=jnp.float32)
    pre_grad = (act_grad * silu_slope(preact)).astype(jnp.bfloat16)
    first_grad = jnp.dot(hidden.T, pre_grad, preferred_element_type=jnp.float32)
    return (cosine.reshape(CLIPS, LENGTH), first_grad.astype(jnp.bfloat16), second_grad.astype(jnp.bfloat16))
```

```python
import functools
import math

import jax
import jax.numpy as jnp
from jax import lax
from jax.experimental import pallas as pl
from jax.experimental.pallas import tpu as pltpu
from jax.sharding import PartitionSpec as P

HEAD_DIM = 64
LANES = 128
EPSILON = 1e-06
SCORE_SCALE = HEAD_DIM ** (-0.5) * math.log2(math.e)
SMALLEST_SUM = 2.0 ** -90
BF16 = jnp.bfloat16
F32 = jnp.float32
NX, NZ, NY = 4, 8, 4


def dp_shift(by):
    return [(i, (i + 2 * by) % (2 * NY)) for i in range(2 * NY)]


def core_swap():
    return [(i, i ^ 1) for i in range(2 * NY)]


def x_shift(by):
    return [(x * NZ + z, ((x + by) % NX) * NZ + z) for x in range(NX) for z in range(NZ)]


def z_shift(by):
    return [(x * NZ + z, x * NZ + (z + by) % NZ) for x in range(NX) for z in range(NZ)]


Z_GROUPS = [[x * NZ + z for z in range(NZ)] for x in range(NX)]


def vmem_spec():
    return pl.BlockSpec(memory_space=pltpu.VMEM)


def params(mib):
    return pltpu.CompilerParams(vmem_limit_bytes=mib * 1024 * 1024)


def pack_kernel(query_ref, key_ref, value_ref, out_ref):
    for row, source in ((0, query_ref), (HEAD_DIM, key_ref), (2 * HEAD_DIM, value_ref)):
        for pair in range(source.shape[1] // LANES):
            turned = source[:, pair * LANES : (pair + 1) * LANES].T
            out_ref[2 * pair, row : row + HEAD_DIM, :] = turned[:HEAD_DIM]
            out_ref[2 * pair + 1, row : row + HEAD_DIM, :] = turned[HEAD_DIM:]


def pack(query, key, value):
    heads = query.shape[1] // HEAD_DIM
    return pl.pallas_call(
        pack_kernel,
        out_shape=jax.ShapeDtypeStruct((heads, 3 * HEAD_DIM, LANES), BF16),
        in_specs=[vmem_spec()] * 3,
        out_specs=vmem_spec(),
        compiler_params=params(32),
        name="pack",
    )(query, key, value)


Q_ROWS = 512
K_ROWS = 1024
DEPTH = 2 * HEAD_DIM + 16
V_ROWS = HEAD_DIM + 16


def attend_kernel(qkv_ref, out_ref, key_buf, value_buf):
    slabs = qkv_ref.shape[0]
    length = slabs * LANES
    per_block = Q_ROWS // LANES
    largest = jnp.zeros((1, LANES), F32)
    for slab in range(slabs):
        rows = slice(slab * LANES, (slab + 1) * LANES)
        keys = qkv_ref[slab, HEAD_DIM : 2 * HEAD_DIM, :]
        turned = keys.T
        key_buf[rows, 0:HEAD_DIM] = turned
        key_buf[rows, HEAD_DIM : 2 * HEAD_DIM] = turned
        wide = keys.astype(F32)
        largest = jnp.maximum(largest, jnp.sum(wide * wide, axis=0, keepdims=True))
        value_buf[0:HEAD_DIM, rows] = qkv_ref[slab, 2 * HEAD_DIM : 3 * HEAD_DIM, :]
    key_buf[:, 2 * HEAD_DIM : DEPTH] = jnp.ones((length, DEPTH - 2 * HEAD_DIM), BF16)
    value_buf[HEAD_DIM:V_ROWS, :] = jnp.ones((V_ROWS - HEAD_DIM, length), BF16)
    key_bound = jnp.max(largest, axis=1, keepdims=True)

    def load_queries(block):
        return jnp.concatenate(
            [qkv_ref[block * per_block + j, 0:HEAD_DIM, :] for j in range(per_block)], axis=1
        )

    def store(block, total):
        result = (total[0:HEAD_DIM] / total[HEAD_DIM : HEAD_DIM + 1]).astype(BF16)
        for j in range(per_block):
            out_ref[block * per_block + j] = result[:, j * LANES : (j + 1) * LANES]

    first_row = lax.broadcasted_iota(jnp.int32, (DEPTH - 2 * HEAD_DIM, Q_ROWS), 0) == 0

    def step(block, least):
        queries = load_queries(block).astype(F32)
        bound = SCORE_SCALE * jnp.sqrt(
            jnp.sum(queries * queries, axis=0, keepdims=True) * key_bound
        )
        scaled = queries * SCORE_SCALE
        high = scaled.astype(BF16)
        low = (scaled - high.astype(F32)).astype(BF16)
        shift = jnp.where(first_row, -bound, 0.0).astype(BF16)
        stacked = jnp.concatenate([high, low, shift], axis=0)
        total = jnp.zeros((V_ROWS, Q_ROWS), F32)
        for part in range(length // K_ROWS):
            span = slice(part * K_ROWS, (part + 1) * K_ROWS)
            scores = jnp.dot(key_buf[span, :], stacked, preferred_element_type=F32)
            weights = jnp.exp2(scores).astype(BF16)
            total = total + jnp.dot(value_buf[:, span], weights, preferred_element_type=F32)
        store(block, total)
        return jnp.minimum(least, total[HEAD_DIM : HEAD_DIM + 1])

    least = lax.fori_loop(0, length // Q_ROWS, step, jnp.full((1, Q_ROWS), 1.0, F32))

    @pl.when(jnp.min(least) < SMALLEST_SUM)
    def _():
        def careful(block, _):
            queries = load_queries(block)

            def inner(part, state):
                top, total = state
                begin = pl.multiple_of(part * K_ROWS, K_ROWS)
                keys = key_buf[pl.ds(begin, K_ROWS), 0:HEAD_DIM]
                scores = jnp.dot(keys, queries, preferred_element_type=F32)
                higher = jnp.maximum(top, jnp.max(scores, axis=0, keepdims=True))
                weights = jnp.exp2((scores - higher) * SCORE_SCALE).astype(BF16)
                fade = jnp.exp2((top - higher) * SCORE_SCALE)
                added = jnp.dot(
                    value_buf[:, pl.ds(begin, K_ROWS)], weights, preferred_element_type=F32
                )
                return higher, total * fade + added

            start = (jnp.full((1, Q_ROWS), -1e30, F32), jnp.zeros((V_ROWS, Q_ROWS), F32))
            _, total = lax.fori_loop(0, length // K_ROWS, inner, start)
            store(block, total)
            return 0

        lax.fori_loop(0, length // Q_ROWS, careful, 0)


def attend(qkv):
    slabs = qkv.shape[0]
    length = slabs * LANES
    return pl.pallas_call(
        attend_kernel,
        out_shape=jax.ShapeDtypeStruct((slabs, HEAD_DIM, LANES), BF16),
        in_specs=[vmem_spec()],
        out_specs=vmem_spec(),
        scratch_shapes=[pltpu.VMEM((length, DEPTH), BF16), pltpu.VMEM((V_ROWS, length), BF16)],
        compiler_params=params(48),
        cost_estimate=pl.CostEstimate(
            flops=4 * length * length * 256, bytes_accessed=2**21, transcendentals=length * length
        ),
        name="attend",
    )(qkv)


def unpack_kernel(place_ref, *refs):
    *parts, first_ref, second_ref = refs
    first_rows = first_ref.shape[0] // NZ
    second_rows = second_ref.shape[0] // NZ
    first_cols = first_ref.shape[1] // NX
    second_cols = second_ref.shape[1] // NX
    for d, part in enumerate(parts):
        column = lax.rem(place_ref[0] + d, NX)
        for z in range(NZ):
            row = 0
            for lane in range(first_cols // LANES):
                begin = pl.multiple_of(column * first_cols + lane * LANES, LANES)
                first_ref[z * first_rows : (z + 1) * first_rows, pl.ds(begin, LANES)] = part[
                    z, row : row + first_rows, :
                ]
                row += first_rows
            for lane in range(second_cols // LANES):
                begin = pl.multiple_of(column * second_cols + lane * LANES, LANES)
                second_ref[z * second_rows : (z + 1) * second_rows, pl.ds(begin, LANES)] = part[
                    z, row : row + second_rows, :
                ]
                row += second_rows


def unpack(place, parts, first_shape, second_shape):
    return pl.pallas_call(
        unpack_kernel,
        out_shape=(
            jax.ShapeDtypeStruct(first_shape, BF16),
            jax.ShapeDtypeStruct(second_shape, BF16),
        ),
        in_specs=[pl.BlockSpec(memory_space=pltpu.SMEM)] + [vmem_spec()] * len(parts),
        out_specs=(vmem_spec(), vmem_spec()),
        compiler_params=params(32),
        name="unpack",
    )(place.reshape(1), *parts)


def contract_rows(left, right):
    return lax.dot_general(left, right, (((0,), (0,)), ((), ())), preferred_element_type=F32)


def body(
    query_in,
    key_in,
    value_in,
    residual,
    out_proj,
    first_proj,
    first_bias,
    second_proj,
    second_bias,
    teacher,
    teach_index,
    teach_weight,
):
    dp = lax.axis_index("dp")
    seq = lax.axis_index("seq")
    y, core = dp // 2, lax.rem(dp, 2)
    x = seq // NZ
    tokens = query_in.shape[1]
    width = residual.shape[2]
    hid = first_bias.shape[0]
    outf = second_bias.shape[0]

    second_full = lax.all_gather(second_proj, "dp", axis=0, tiled=True)
    swap = functools.partial(lax.ppermute, axis_name="dp", perm=core_swap())
    out_wide = jnp.concatenate([out_proj, swap(out_proj)], axis=1)
    first_wide = jnp.concatenate([first_proj, swap(first_proj)], axis=0)
    by_core = residual.reshape(NY, 2, tokens, width)
    mine = lax.dynamic_index_in_dim(by_core, core, 1, keepdims=False)
    theirs = lax.dynamic_index_in_dim(by_core, 1 - core, 1, keepdims=False)
    residual_wide = jnp.concatenate([mine, swap(theirs)], axis=2)

    local = teacher[0]
    rows = local.shape[0]
    count = lax.axis_size("seq")
    before = lax.ppermute(local, "seq", [(i, i + 1) for i in range(count - 1)])
    after = lax.ppermute(local, "seq", [(i + 1, i) for i in range(count - 1)])
    window = jnp.concatenate([before, local, after], axis=0)
    offsets = teach_index - (seq - 1) * rows
    spots = jnp.arange(3 * rows, dtype=jnp.int32)
    blend = jnp.sum(
        jnp.where(offsets[:, :, None] == spots, teach_weight[:, :, None], 0.0), axis=1
    )
    target = jnp.dot(blend, window.astype(F32), precision=lax.Precision.HIGHEST)

    qkv = lax.all_to_all(
        pack(query_in[0], key_in[0], value_in[0]), "seq", 0, 0, tiled=True
    )
    attended = lax.all_to_all(attend(qkv), "seq", 0, 0, tiled=True)
    attended = attended.reshape(-1, tokens)

    order = (0, 1, 3, 2)
    hidden = {}
    partial = {}
    for r in order:
        block = attended if r == 0 else lax.ppermute(attended, "dp", dp_shift(-r))
        mixed = contract_rows(block, out_wide)
        rows_r = lax.dynamic_index_in_dim(
            residual_wide, lax.rem(y + r, NY), 0, keepdims=False
        )
        hidden[r] = (rows_r + mixed).astype(BF16)
        terms = jnp.dot(hidden[r], first_wide, preferred_element_type=F32).astype(BF16)
        partial[r] = terms if r == 0 else lax.ppermute(terms, "dp", dp_shift(r))
    preact = first_bias + sum(partial[r].astype(F32) for r in order)

    hidden_own = jnp.concatenate([hidden[r] for r in range(NY)], axis=0)
    hidden_x = [hidden_own if d == 0 else lax.ppermute(hidden_own, "seq", x_shift(-d)) for d in range(NX)]

    gate = jax.nn.sigmoid(preact)
    activated = (preact * gate).astype(BF16)
    slope = gate * (1.0 + preact * (1.0 - gate))
    chip_units = hid // NY
    activated_y = []
    for r in range(NY):
        part = lax.dynamic_slice_in_dim(
            activated, lax.rem(y - r + NY, NY) * chip_units, chip_units, axis=1
        )
        activated_y.append(part if r == 0 else lax.ppermute(part, "dp", dp_shift(-r)))
    projected = jnp.dot(activated, second_full, preferred_element_type=F32) + second_bias
    inv_model = lax.rsqrt(jnp.sum(projected * projected, axis=1, keepdims=True) + EPSILON)
    inv_target = lax.rsqrt(jnp.sum(target * target, axis=1, keepdims=True) + EPSILON)
    cosine = jnp.sum(projected * target, axis=1, keepdims=True) * inv_model * inv_target
    row_grad = (
        -math.sqrt(outf) * inv_model * (target * inv_target - cosine * inv_model * projected)
    ).astype(BF16)
    back = lax.dot_general(
        row_grad, second_full, (((1,), (1,)), ((), ())), preferred_element_type=F32
    )
    pre_grad = (back * slope).astype(BF16)

    row_grad_y = [row_grad if r == 0 else lax.ppermute(row_grad, "dp", dp_shift(-r)) for r in range(NY)]
    second_chip = sum(contract_rows(a, g) for a, g in zip(activated_y, row_grad_y))
    units = second_proj.shape[0]
    second_cores = second_chip.astype(BF16).reshape(2, units, outf)
    second_own = (
        lax.dynamic_index_in_dim(second_cores, core, 0, keepdims=False).astype(F32)
        + swap(lax.dynamic_index_in_dim(second_cores, 1 - core, 0, keepdims=False)).astype(F32)
    ).astype(BF16)
    second_cols = outf // NX
    second_sum = 0.0
    for d in range(NX):
        part = lax.dynamic_slice_in_dim(
            second_own, lax.rem(x - d + NX, NX) * second_cols, second_cols, axis=1
        )
        if d:
            part = lax.ppermute(part, "seq", x_shift(-d))
        second_sum = second_sum + part.astype(F32)
    second_sum = second_sum.astype(BF16)

    first_cols = hid // NX
    pre_x = []
    for d in range(NX):
        part = lax.dynamic_slice_in_dim(
            pre_grad, lax.rem(x - d + NX, NX) * first_cols, first_cols, axis=1
        )
        pre_x.append(part if d == 0 else lax.ppermute(part, "seq", x_shift(-d)))
    pre_x = jnp.stack(pre_x)
    first_chip = 0.0
    for r in order:
        block = pre_x if r == 0 else lax.ppermute(pre_x, "dp", dp_shift(-r))
        left = jnp.concatenate(
            [hidden_x[d][r * tokens : (r + 1) * tokens] for d in range(NX)], axis=0
        )
        first_chip = first_chip + contract_rows(left, block.reshape(-1, first_cols))
    first_chip = first_chip.astype(BF16)
    first_sum = (
        first_chip[:width].astype(F32) + swap(first_chip[width:]).astype(F32)
    ).astype(BF16)

    first_rows = width // NZ
    second_rows = units // NZ
    packed = jnp.concatenate(
        [
            first_sum.reshape(NZ, first_rows, -1, LANES).transpose(0, 2, 1, 3).reshape(NZ, -1, LANES),
            second_sum.reshape(NZ, second_rows, -1, LANES).transpose(0, 2, 1, 3).reshape(NZ, -1, LANES),
        ],
        axis=1,
    )
    pieces = lax.all_to_all(packed, "seq", 0, 0, tiled=True, axis_index_groups=Z_GROUPS)
    summed = jnp.sum(pieces.astype(F32), axis=0).astype(BF16)
    column = lax.all_gather(summed, "seq", axis=0, axis_index_groups=Z_GROUPS)
    columns = [column if d == 0 else lax.ppermute(column, "seq", x_shift(-d)) for d in range(NX)]
    grad_first, grad_second = unpack(x, columns, (width, hid), (units, outf))
    return (cosine.reshape(1, -1), grad_first, grad_second)


def solution(mesh):
    placed = (
        P("dp", "seq", None),
        P("dp", "seq", None),
        P("dp", "seq", None),
        P(None, "seq", "dp"),
        P(None, "dp"),
        P("dp", None),
        P(),
        P("dp", None),
        P(),
        P("dp", "seq", None),
        P("seq", None),
        P("seq", None),
    )
    return jax.shard_map(
        body,
        mesh=mesh,
        in_specs=placed,
        out_specs=(P("dp", "seq"), P("dp", None), P("dp", None)),
        check_vma=False,
    )
```

```python
import functools
import math

import jax
import jax.numpy as jnp
from jax import lax
from jax.experimental import pallas as pl
from jax.experimental.pallas import tpu as pltpu
from jax.sharding import PartitionSpec as P

HEAD_DIM = 64
LANES = 128
EPSILON = 1e-06
SCORE_SCALE = HEAD_DIM ** (-0.5) * math.log2(math.e)
SMALLEST_SUM = 2.0 ** -90
BF16 = jnp.bfloat16
F32 = jnp.float32
NX, NZ, NY = 4, 8, 4
SMALL = pl.CostEstimate(flops=0, bytes_accessed=0, transcendentals=0)


def dp_shift(by):
    return [(i, (i + 2 * by) % (2 * NY)) for i in range(2 * NY)]


def core_swap():
    return [(i, i ^ 1) for i in range(2 * NY)]


def x_shift(by):
    return [(x * NZ + z, ((x + by) % NX) * NZ + z) for x in range(NX) for z in range(NZ)]


def z_swap():
    return [(i, i ^ 1) for i in range(NX * NZ)]


X_GROUPS = [[x * NZ + z for x in range(NX)] for z in range(NZ)]
PARITY_GROUPS = [
    [x * NZ + 2 * pair + parity for pair in range(NZ // 2)]
    for x in range(NX)
    for parity in range(2)
]


def vmem_spec():
    return pl.BlockSpec(memory_space=pltpu.VMEM)


def params(mib):
    return pltpu.CompilerParams(vmem_limit_bytes=mib * 1024 * 1024)


def pack_kernel(query_hbm, key_hbm, value_hbm, out_hbm, in_buf, out_buf, in_sems, out_sems):
    steps = in_sems.shape[0]
    cols = in_buf.shape[2] // steps
    heads = out_buf.shape[0] // steps
    loads = [
        [
            pltpu.make_async_copy(
                source.at[:, pl.ds(step * cols, cols)],
                in_buf.at[which, :, pl.ds(step * cols, cols)],
                in_sems.at[step, which],
            )
            for which, source in enumerate((query_hbm, key_hbm, value_hbm))
        ]
        for step in range(steps)
    ]
    stores = [
        pltpu.make_async_copy(
            out_buf.at[pl.ds(step * heads, heads)],
            out_hbm.at[pl.ds(step * heads, heads)],
            out_sems.at[step],
        )
        for step in range(steps)
    ]
    for step in range(steps):
        for load in loads[step]:
            load.start()
    for step in range(steps):
        for which, load in enumerate(loads[step]):
            load.wait()
            row = which * HEAD_DIM
            for pair in range(step * heads // 2, (step + 1) * heads // 2):
                turned = in_buf[which, :, pair * LANES : (pair + 1) * LANES].T
                out_buf[2 * pair, row : row + HEAD_DIM, :] = turned[:HEAD_DIM]
                out_buf[2 * pair + 1, row : row + HEAD_DIM, :] = turned[HEAD_DIM:]
        stores[step].start()
    for store in stores:
        store.wait()


def pack(query, key, value):
    tokens, width = query.shape
    heads = width // HEAD_DIM
    steps = 4
    hbm = pl.BlockSpec(memory_space=pltpu.HBM)
    return pl.pallas_call(
        pack_kernel,
        out_shape=jax.ShapeDtypeStruct((heads, 3 * HEAD_DIM, tokens), BF16),
        in_specs=[hbm] * 3,
        out_specs=hbm,
        scratch_shapes=[
            pltpu.VMEM((3, tokens, width), BF16),
            pltpu.VMEM((heads, 3 * HEAD_DIM, tokens), BF16),
            pltpu.SemaphoreType.DMA((steps, 3)),
            pltpu.SemaphoreType.DMA((steps,)),
        ],
        compiler_params=params(56),
        cost_estimate=SMALL,
        name="pack",
    )(query, key, value)


Q_ROWS = 512
K_ROWS = 1024
DEPTH = 2 * HEAD_DIM + 16
V_ROWS = HEAD_DIM + 16


def attend_kernel(qkv_ref, out_ref, key_buf, value_buf):
    slabs = qkv_ref.shape[0]
    length = slabs * LANES
    per_block = Q_ROWS // LANES
    largest = jnp.zeros((1, LANES), F32)
    for slab in range(slabs):
        rows = slice(slab * LANES, (slab + 1) * LANES)
        keys = qkv_ref[slab, HEAD_DIM : 2 * HEAD_DIM, :]
        turned = keys.T
        key_buf[rows, 0:HEAD_DIM] = turned
        key_buf[rows, HEAD_DIM : 2 * HEAD_DIM] = turned
        wide = keys.astype(F32)
        largest = jnp.maximum(largest, jnp.sum(wide * wide, axis=0, keepdims=True))
        value_buf[0:HEAD_DIM, rows] = qkv_ref[slab, 2 * HEAD_DIM : 3 * HEAD_DIM, :]
    key_buf[:, 2 * HEAD_DIM : DEPTH] = jnp.ones((length, DEPTH - 2 * HEAD_DIM), BF16)
    value_buf[HEAD_DIM:V_ROWS, :] = jnp.ones((V_ROWS - HEAD_DIM, length), BF16)
    key_bound = jnp.max(largest, axis=1, keepdims=True)

    def load_queries(block):
        return jnp.concatenate(
            [qkv_ref[block * per_block + j, 0:HEAD_DIM, :] for j in range(per_block)], axis=1
        )

    def store(block, total):
        result = (total[0:HEAD_DIM] / total[HEAD_DIM : HEAD_DIM + 1]).astype(BF16)
        for j in range(per_block):
            out_ref[block * per_block + j] = result[:, j * LANES : (j + 1) * LANES]

    first_row = lax.broadcasted_iota(jnp.int32, (DEPTH - 2 * HEAD_DIM, Q_ROWS), 0) == 0

    def step(block, least):
        queries = load_queries(block).astype(F32)
        bound = SCORE_SCALE * jnp.sqrt(
            jnp.sum(queries * queries, axis=0, keepdims=True) * key_bound
        )
        scaled = queries * SCORE_SCALE
        high = scaled.astype(BF16)
        low = (scaled - high.astype(F32)).astype(BF16)
        shift = jnp.where(first_row, -bound, 0.0).astype(BF16)
        stacked = jnp.concatenate([high, low, shift], axis=0)
        total = jnp.zeros((V_ROWS, Q_ROWS), F32)
        for part in range(length // K_ROWS):
            span = slice(part * K_ROWS, (part + 1) * K_ROWS)
            scores = jnp.dot(key_buf[span, :], stacked, preferred_element_type=F32)
            weights = jnp.exp2(scores).astype(BF16)
            total = total + jnp.dot(value_buf[:, span], weights, preferred_element_type=F32)
        store(block, total)
        return jnp.minimum(least, total[HEAD_DIM : HEAD_DIM + 1])

    least = lax.fori_loop(0, length // Q_ROWS, step, jnp.full((1, Q_ROWS), 1.0, F32))

    @pl.when(jnp.min(least) < SMALLEST_SUM)
    def _():
        def careful(block, _):
            queries = load_queries(block)

            def inner(part, state):
                top, total = state
                begin = pl.multiple_of(part * K_ROWS, K_ROWS)
                keys = key_buf[pl.ds(begin, K_ROWS), 0:HEAD_DIM]
                scores = jnp.dot(keys, queries, preferred_element_type=F32)
                higher = jnp.maximum(top, jnp.max(scores, axis=0, keepdims=True))
                weights = jnp.exp2((scores - higher) * SCORE_SCALE).astype(BF16)
                fade = jnp.exp2((top - higher) * SCORE_SCALE)
                added = jnp.dot(
                    value_buf[:, pl.ds(begin, K_ROWS)], weights, preferred_element_type=F32
                )
                return higher, total * fade + added

            start = (jnp.full((1, Q_ROWS), -1e30, F32), jnp.zeros((V_ROWS, Q_ROWS), F32))
            _, total = lax.fori_loop(0, length // K_ROWS, inner, start)
            store(block, total)
            return 0

        lax.fori_loop(0, length // Q_ROWS, careful, 0)


def attend(qkv):
    slabs = qkv.shape[0]
    length = slabs * LANES
    return pl.pallas_call(
        attend_kernel,
        out_shape=jax.ShapeDtypeStruct((slabs, HEAD_DIM, LANES), BF16),
        in_specs=[vmem_spec()],
        out_specs=vmem_spec(),
        scratch_shapes=[pltpu.VMEM((length, DEPTH), BF16), pltpu.VMEM((V_ROWS, length), BF16)],
        compiler_params=params(20),
        cost_estimate=SMALL,
        name="attend",
    )(qkv)


def stage(sources, buffers, sems):
    copies = [
        pltpu.make_async_copy(source, buffer, sems.at[i])
        for i, (source, buffer) in enumerate(zip(sources, buffers))
    ]
    for copy in copies:
        copy.start()
    return copies


def hidden_kernel(pieces, y_ref, *refs):
    arrays = sum(count for _, count in pieces)
    clips = len(pieces)
    parts, refs = refs[:arrays], refs[arrays:]
    residual, out_hbm, first_hbm = refs[:3]
    hidden_ref, *terms = refs[3 : 4 + clips]
    rows_buf, residual_buf, out_buf, first_buf, sems = refs[4 + clips :]
    inner = out_buf.shape[0]
    chunks = 4
    depth = inner // chunks
    span = first_buf.shape[0] // 2
    sources = list(parts) + [residual]
    buffers = []
    for clip, (_, count) in enumerate(pieces):
        size = inner // count
        buffers += [rows_buf.at[clip, pl.ds(k * size, size)] for k in range(count)]
    buffers.append(residual_buf)
    for k in range(chunks):
        sources.append(out_hbm.at[pl.ds(k * depth, depth)])
        buffers.append(out_buf.at[pl.ds(k * depth, depth)])
    for k in range(2):
        sources.append(first_hbm.at[pl.ds(k * span, span)])
        buffers.append(first_buf.at[pl.ds(k * span, span)])
    copies = stage(sources, buffers, sems)
    for copy in copies[: arrays + 1]:
        copy.wait()
    tokens = rows_buf.shape[2]
    mixed = jnp.concatenate(
        [residual_buf[lax.rem(y_ref[0] + r, NY)].astype(F32) for r, _ in pieces], axis=0
    )
    for k in range(chunks):
        part = slice(k * depth, (k + 1) * depth)
        rows = jnp.concatenate([rows_buf[clip, part, :].T for clip in range(clips)], axis=0)
        copies[arrays + 1 + k].wait()
        mixed = mixed + jnp.dot(rows, out_buf[part, :], preferred_element_type=F32)
    hidden = mixed.astype(BF16)
    for copy in copies[arrays + 1 + chunks :]:
        copy.wait()
    for clip, ref in enumerate(terms):
        rows = hidden[clip * tokens : (clip + 1) * tokens]
        hidden_ref[clip] = rows
        ref[...] = jnp.dot(rows, first_buf[...], preferred_element_type=F32).astype(BF16)


def hidden_rows(pieces, y, parts, residual, out_wide, first_wide):
    inner = out_wide.shape[0]
    tokens = parts[0].shape[1]
    width, hid = first_wide.shape
    clips = len(pieces)
    return pl.pallas_call(
        functools.partial(hidden_kernel, pieces),
        out_shape=(
            jax.ShapeDtypeStruct((clips, tokens, width), BF16),
            *[jax.ShapeDtypeStruct((tokens, hid), BF16)] * clips,
        ),
        in_specs=[pl.BlockSpec(memory_space=pltpu.SMEM)]
        + [pl.BlockSpec(memory_space=pl.ANY)] * (3 + len(parts)),
        out_specs=(vmem_spec(),) * (1 + clips),
        scratch_shapes=[
            pltpu.VMEM((clips, inner, tokens), BF16),
            pltpu.VMEM((NY, tokens, width), BF16),
            pltpu.VMEM((inner, width), BF16),
            pltpu.VMEM((width, hid), BF16),
            pltpu.SemaphoreType.DMA((len(parts) + 7,)),
        ],
        compiler_params=params(56),
        cost_estimate=SMALL,
        name="hidden",
    )(y.reshape(1), *parts, residual, out_wide, first_wide)


def similar_kernel(
    place_ref, own_hbm, one_hbm, two_hbm, three_hbm, target_hbm, second_hbm, first_bias_ref,
    second_bias_ref, send_0, send_1, send_2, send_3, pre_grad_ref, cosine_ref,
    terms_ref, target_ref, second_ref, active_ref, slope_ref, sems,
):
    hid, outf = second_ref.shape
    chunks = 4
    depth = hid // chunks
    sources = [own_hbm, one_hbm, two_hbm, three_hbm]
    buffers = [terms_ref.at[r] for r in range(NY)]
    for k in range(chunks):
        sources.append(second_hbm.at[pl.ds(k * depth, depth)])
        buffers.append(second_ref.at[pl.ds(k * depth, depth)])
    copies = stage(sources + [target_hbm], buffers + [target_ref], sems)
    for copy in copies[:NY]:
        copy.wait()
    preact = first_bias_ref[...] + sum(terms_ref[r].astype(F32) for r in range(NY))
    gate = 1.0 / (1.0 + jnp.exp(-preact))
    active_ref[...] = (preact * gate).astype(BF16)
    slope_ref[...] = gate * (1.0 + preact * (1.0 - gate))
    projected = jnp.broadcast_to(second_bias_ref[...], target_ref.shape)
    for k in range(chunks):
        copies[NY + k].wait()
        span = slice(k * depth, (k + 1) * depth)
        projected = projected + jnp.dot(
            active_ref[:, span], second_ref[span, :], preferred_element_type=F32
        )
    copies[-1].wait()
    target = target_ref[...]
    inv_model = lax.rsqrt(jnp.sum(projected * projected, axis=1, keepdims=True) + EPSILON)
    inv_target = lax.rsqrt(jnp.sum(target * target, axis=1, keepdims=True) + EPSILON)
    cosine = jnp.sum(projected * target, axis=1, keepdims=True) * inv_model * inv_target
    cosine_ref[...] = cosine
    row_grad = (
        -math.sqrt(outf) * inv_model * (target * inv_target - cosine * inv_model * projected)
    ).astype(BF16)
    units = hid // NY
    for r, send in enumerate((send_0, send_1, send_2, send_3)):
        chip = lax.rem(place_ref[0] + (NY - r), NY)
        send[:, :units] = active_ref[:, pl.ds(pl.multiple_of(chip * units, units), units)]
        send[:, units:] = row_grad
    cols = hid // NX
    for quarter in range(NX):
        span = slice(quarter * cols, (quarter + 1) * cols)
        back = lax.dot_general(
            row_grad, second_ref[span, :], (((1,), (1,)), ((), ())), preferred_element_type=F32
        )
        pre_grad_ref[quarter] = (back * slope_ref[:, span]).astype(BF16)


def similar(y, terms, first_bias, second_full, second_bias, target):
    tokens, hid = terms[0].shape
    outf = second_full.shape[1]
    send = jax.ShapeDtypeStruct((tokens, hid // NY + outf), BF16)
    specs = [pl.BlockSpec(memory_space=pl.ANY)] * (NY + 2) + [vmem_spec()] * 2
    return pl.pallas_call(
        similar_kernel,
        out_shape=(
            (send,) * NY
            + (
                jax.ShapeDtypeStruct((NX, tokens, hid // NX), BF16),
                jax.ShapeDtypeStruct((tokens, 1), F32),
            )
        ),
        in_specs=[pl.BlockSpec(memory_space=pltpu.SMEM)] + specs,
        out_specs=(vmem_spec(),) * (NY + 2),
        scratch_shapes=[
            pltpu.VMEM((NY, tokens, hid), BF16),
            pltpu.VMEM((tokens, outf), F32),
            pltpu.VMEM((hid, outf), BF16),
            pltpu.VMEM((tokens, hid), BF16),
            pltpu.VMEM((tokens, hid), F32),
            pltpu.SemaphoreType.DMA((NY + 5,)),
        ],
        compiler_params=params(56),
        cost_estimate=SMALL,
        name="similar",
    )(
        y.reshape(1), *terms, target, second_full, first_bias.reshape(1, -1),
        second_bias.reshape(1, -1),
    )


def second_kernel(core_ref, one, two, three, four, keep_ref, give_ref):
    units = 2 * keep_ref.shape[1]
    cols = keep_ref.shape[2]
    parts = (one, two, three, four)
    active = jnp.concatenate([part[:, :units] for part in parts], axis=0).T
    grads = [
        jnp.concatenate(
            [part[:, units + x * cols : units + (x + 1) * cols] for part in parts], axis=0
        )
        for x in range(NX)
    ]
    half = units // 2
    for x in range(NX):
        total = jnp.dot(active, grads[x], preferred_element_type=F32).astype(BF16)
        top, bottom = total[:half], total[half:]
        first = core_ref[0] == 0
        keep_ref[x] = jnp.where(first, top, bottom)
        give_ref[x] = jnp.where(first, bottom, top)


def second_gradient(core, parts, units, outf):
    shape = jax.ShapeDtypeStruct((NX, units, outf // NX), BF16)
    return pl.pallas_call(
        second_kernel,
        out_shape=(shape, shape),
        in_specs=[pl.BlockSpec(memory_space=pltpu.SMEM)] + [vmem_spec()] * NY,
        out_specs=(vmem_spec(), vmem_spec()),
        compiler_params=params(24),
        cost_estimate=SMALL,
        name="second",
    )(core.reshape(1), *parts)


def first_kernel(clips, hidden_hbm, *refs):
    arrays = sum(count for _, count in clips)
    parts, refs = refs[:arrays], refs[arrays:]
    *before, total_ref, hidden_buf, grad_buf, sems = refs
    sources = []
    buffers = []
    for i, (r, count) in enumerate(clips):
        sources.append(hidden_hbm.at[:, r])
        buffers.append(hidden_buf.at[i])
        size = NX // count
        buffers += [grad_buf.at[i, pl.ds(k * size, size)] for k in range(count)]
        sources += parts[:count]
        parts = parts[count:]
    copies = stage(sources, buffers, sems)
    total = before[0][...] if before else 0.0
    for i, (_, count) in enumerate(clips):
        for copy in copies[: count + 1]:
            copy.wait()
        copies = copies[count + 1 :]
        left = hidden_buf[i].reshape(-1, hidden_buf.shape[3])
        right = grad_buf[i].reshape(-1, grad_buf.shape[3])
        total = total + jnp.dot(left.T, right, preferred_element_type=F32)
    total_ref[...] = total.astype(total_ref.dtype)


def first_gradient(clips, hidden, grads, before, kind):
    _, _, tokens, width = hidden.shape
    cols = grads[0].shape[2]
    return pl.pallas_call(
        functools.partial(first_kernel, clips),
        out_shape=jax.ShapeDtypeStruct((width, cols), kind),
        in_specs=[pl.BlockSpec(memory_space=pl.ANY)] * (1 + len(grads))
        + [vmem_spec()] * len(before),
        out_specs=vmem_spec(),
        scratch_shapes=[
            pltpu.VMEM((len(clips), NX, tokens, width), BF16),
            pltpu.VMEM((len(clips), NX, tokens, cols), BF16),
            pltpu.SemaphoreType.DMA((len(clips) + len(grads),)),
        ],
        compiler_params=params(56),
        cost_estimate=SMALL,
        name="first",
    )(hidden, *grads, *before)


def arrange_kernel(own_ref, other_ref, second_ref, out_ref):
    first = own_ref[...].astype(F32) + other_ref[...].astype(F32)
    second = second_ref[0].astype(F32)
    for x in range(1, NX):
        second = second + second_ref[x].astype(F32)
    for z in range(NZ):
        row = 0
        for total in (first.astype(BF16), second.astype(BF16)):
            rows = total.shape[0] // NZ
            for lane in range(total.shape[1] // LANES):
                out_ref[z // 2, z % 2, row : row + rows, :] = total[
                    z * rows : (z + 1) * rows, lane * LANES : (lane + 1) * LANES
                ]
                row += rows


def arrange(own, other, second):
    rows = (own.size + second[0].size) // (NZ * LANES)
    return pl.pallas_call(
        arrange_kernel,
        out_shape=jax.ShapeDtypeStruct((NZ // 2, 2, rows, LANES), BF16),
        in_specs=[vmem_spec()] * 3,
        out_specs=vmem_spec(),
        compiler_params=params(16),
        cost_estimate=SMALL,
        name="arrange",
    )(own, other, second)


def part_kernel(parity_ref, blocks_ref, keep_ref, give_ref):
    for index, ref in ((parity_ref[0], keep_ref), (1 - parity_ref[0], give_ref)):
        total = blocks_ref[0, index].astype(F32)
        for pair in range(1, NZ // 2):
            total = total + blocks_ref[pair, index].astype(F32)
        ref[...] = total.astype(ref.dtype)


def part(parity, blocks):
    return pl.pallas_call(
        part_kernel,
        out_shape=(
            jax.ShapeDtypeStruct(blocks.shape[2:], F32),
            jax.ShapeDtypeStruct(blocks.shape[2:], BF16),
        ),
        in_specs=[pl.BlockSpec(memory_space=pltpu.SMEM), vmem_spec()],
        out_specs=(vmem_spec(), vmem_spec()),
        compiler_params=params(16),
        cost_estimate=SMALL,
        name="part",
    )(parity.reshape(1), blocks)


def unpack_kernel(place_ref, *refs):
    *parts, first_ref, second_ref = refs
    for index, part in enumerate(parts):
        column = lax.rem(place_ref[0] + index // 2, NX)
        parity = lax.rem(place_ref[1] + index % 2, 2)
        for pair in range(NZ // 2):
            z = 2 * pair + parity
            row = 0
            for ref in (first_ref, second_ref):
                rows = ref.shape[0] // NZ
                cols = ref.shape[1] // NX
                to_row = pl.multiple_of(z * rows, rows)
                for lane in range(cols // LANES):
                    to_lane = pl.multiple_of(column * cols + lane * LANES, LANES)
                    ref[pl.ds(to_row, rows), pl.ds(to_lane, LANES)] = part[
                        pair, row : row + rows, :
                    ]
                    row += rows


def unpack(place, parts, first_shape, second_shape):
    return pl.pallas_call(
        unpack_kernel,
        out_shape=(
            jax.ShapeDtypeStruct(first_shape, BF16),
            jax.ShapeDtypeStruct(second_shape, BF16),
        ),
        in_specs=[pl.BlockSpec(memory_space=pltpu.SMEM)] + [vmem_spec()] * len(parts),
        out_specs=(vmem_spec(), vmem_spec()),
        compiler_params=params(16),
        cost_estimate=SMALL,
        name="unpack",
    )(place, *parts)


def after(values, *others):
    return lax.optimization_barrier((values, others))[0]


def body(
    query_in,
    key_in,
    value_in,
    residual,
    out_proj,
    first_proj,
    first_bias,
    second_proj,
    second_bias,
    teacher,
    teach_index,
    teach_weight,
):
    dp = lax.axis_index("dp")
    seq = lax.axis_index("seq")
    y, core = dp // 2, lax.rem(dp, 2)
    x = seq // NZ
    tokens = query_in.shape[1]
    width = residual.shape[2]
    hid = first_bias.shape[0]
    outf = second_bias.shape[0]

    second_full = lax.all_gather(second_proj, "dp", axis=0, tiled=True)
    swap = functools.partial(lax.ppermute, axis_name="dp", perm=core_swap())
    out_wide = jnp.concatenate([out_proj, swap(out_proj)], axis=1)
    first_wide = jnp.concatenate([first_proj, swap(first_proj)], axis=0)
    by_core = residual.reshape(NY, 2, tokens, width)
    mine = lax.dynamic_index_in_dim(by_core, core, 1, keepdims=False)
    theirs = lax.dynamic_index_in_dim(by_core, 1 - core, 1, keepdims=False)
    residual_wide = jnp.concatenate([mine, swap(theirs)], axis=2)

    local = teacher[0]
    rows = local.shape[0]
    count = lax.axis_size("seq")
    earlier = lax.ppermute(local, "seq", [(i, i + 1) for i in range(count - 1)])
    later = lax.ppermute(local, "seq", [(i + 1, i) for i in range(count - 1)])
    window = jnp.concatenate([earlier, local, later], axis=0)
    offsets = teach_index - (seq - 1) * rows
    spots = jnp.arange(3 * rows, dtype=jnp.int32)
    blend = jnp.sum(
        jnp.where(offsets[:, :, None] == spots, teach_weight[:, :, None], 0.0), axis=1
    )
    target = jnp.dot(blend, window.astype(F32), precision=lax.Precision.HIGHEST)

    qkv = lax.all_to_all(
        pack(query_in[0], key_in[0], value_in[0]), "seq", 0, 0, tiled=True
    )
    qkv = after(qkv, out_wide, first_wide, residual_wide, second_full)
    attended = lax.all_to_all(attend(qkv), "seq", 0, 0, tiled=True)
    attended = after(attended.reshape(-1, tokens), target)

    def from_y(value, by):
        return lax.ppermute(value, "dp", dp_shift(-by))

    def from_x(value, by):
        return lax.ppermute(value, "seq", x_shift(-by))

    def gather_x(value):
        return lax.all_gather(value, "seq", axis=0, axis_index_groups=X_GROUPS)

    half = attended.shape[0] // 2
    upper = from_y(attended, 1)
    lower = from_y(attended, 3)
    across = [from_y(upper[:half], 1), from_y(lower[half:], 3)]
    near, *near_terms = hidden_rows(
        ((0, 1), (1, 1), (3, 1)), y, [attended, upper, lower], residual_wide, out_wide, first_wide
    )
    across = after(across, near)
    far, far_term = hidden_rows(((2, 2),), y, across, residual_wide, out_wide, first_wide)
    terms = [
        near_terms[0],
        lax.ppermute(near_terms[1], "dp", dp_shift(1)),
        lax.ppermute(far_term, "dp", dp_shift(2)),
        lax.ppermute(near_terms[2], "dp", dp_shift(3)),
    ]

    hidden_x = gather_x(jnp.concatenate([near[:2], far, near[2:]], axis=0))

    *sends, pre_grad, cosine = similar(
        y, terms, first_bias, second_full, second_bias, target
    )
    sends = [sends[0]] + [from_y(sends[r], r) for r in range(1, NY)]

    pre_x = lax.all_to_all(pre_grad, "seq", 0, 0, tiled=True, axis_index_groups=X_GROUPS)
    upper = from_y(pre_x, 1)
    lower = from_y(pre_x, 3)
    across = [from_y(upper[: NX // 2], 1), from_y(lower[NX // 2 :], 3)]

    units = second_proj.shape[0]
    keep, give = second_gradient(core, after(sends, pre_x), units, outf)
    second_own = (keep.astype(F32) + swap(give).astype(F32)).astype(BF16)
    second_parts = lax.all_to_all(
        second_own, "seq", 0, 0, tiled=True, axis_index_groups=X_GROUPS
    )
    across, second_parts = lax.optimization_barrier((across, second_parts))
    total = first_gradient(((1, 1), (3, 1), (0, 1)), hidden_x, [upper, lower, pre_x], [], F32)
    first_chip = first_gradient(((2, 2),), hidden_x, across, [total], BF16)
    first_other = swap(first_chip[width:])

    z = lax.rem(seq, NZ)
    blocks = arrange(first_chip[:width], first_other, second_parts)
    blocks = lax.all_to_all(blocks, "seq", 0, 0, tiled=True, axis_index_groups=PARITY_GROUPS)
    keep, give = part(lax.rem(z, 2), blocks)
    summed = (keep + lax.ppermute(give, "seq", z_swap()).astype(F32)).astype(BF16)

    same = lax.all_gather(summed, "seq", axis=0, axis_index_groups=PARITY_GROUPS)
    other = lax.ppermute(same, "seq", z_swap())
    same_x = {0: same, 1: from_x(same, 1), 3: from_x(same, 3)}
    other_x = {0: other, 1: from_x(other, 1), 3: from_x(other, 3)}
    same_x[2] = from_x(same_x[1], 1)
    other_x[2] = from_x(other_x[3], 3)
    grad_first, grad_second = unpack(
        jnp.stack([x, z]),
        [part for d in range(NX) for part in (same_x[d], other_x[d])],
        (width, hid),
        (units, outf),
    )
    return (cosine.reshape(1, -1), grad_first, grad_second)


def solution(mesh):
    placed = (
        P("dp", "seq", None),
        P("dp", "seq", None),
        P("dp", "seq", None),
        P(None, "seq", "dp"),
        P(None, "dp"),
        P("dp", None),
        P(),
        P("dp", None),
        P(),
        P("dp", "seq", None),
        P("seq", None),
        P("seq", None),
    )
    return jax.shard_map(
        body,
        mesh=mesh,
        in_specs=placed,
        out_specs=(P("dp", "seq"), P("dp", None), P("dp", None)),
        check_vma=False,
    )
```

```python
import functools
import math

import jax
import jax.numpy as jnp
from jax import lax
from jax.experimental import pallas as pl
from jax.experimental.pallas import tpu as pltpu
from jax.sharding import PartitionSpec as P

HEAD_DIM = 64
LANES = 128
EPSILON = 1e-06
SCORE_SCALE = HEAD_DIM ** (-0.5) * math.log2(math.e)
SMALLEST_SUM = 2.0 ** -90
BF16 = jnp.bfloat16
F32 = jnp.float32
NX, NZ, NY = 4, 8, 4
LARGE = pl.CostEstimate(flops=2**35, bytes_accessed=2**23, transcendentals=0)
SMALL = pl.CostEstimate(flops=0, bytes_accessed=0, transcendentals=0)


def dp_shift(by):
    return [(i, (i + 2 * by) % (2 * NY)) for i in range(2 * NY)]


def core_swap():
    return [(i, i ^ 1) for i in range(2 * NY)]


def x_shift(by):
    return [(x * NZ + z, ((x + by) % NX) * NZ + z) for x in range(NX) for z in range(NZ)]


def z_swap():
    return [(i, i ^ 1) for i in range(NX * NZ)]


X_GROUPS = [[x * NZ + z for x in range(NX)] for z in range(NZ)]
PARITY_GROUPS = [
    [x * NZ + 2 * pair + parity for pair in range(NZ // 2)]
    for x in range(NX)
    for parity in range(2)
]


def vmem_spec():
    return pl.BlockSpec(memory_space=pltpu.VMEM)


def params(mib):
    return pltpu.CompilerParams(vmem_limit_bytes=mib * 1024 * 1024)


def pack_kernel(query_hbm, key_hbm, value_hbm, out_hbm, in_buf, out_buf, in_sems, out_sems):
    steps = in_sems.shape[0]
    cols = in_buf.shape[2] // steps
    heads = out_buf.shape[0] // steps
    loads = [
        [
            pltpu.make_async_copy(
                source.at[:, pl.ds(step * cols, cols)],
                in_buf.at[which, :, pl.ds(step * cols, cols)],
                in_sems.at[step, which],
            )
            for which, source in enumerate((query_hbm, key_hbm, value_hbm))
        ]
        for step in range(steps)
    ]
    stores = [
        pltpu.make_async_copy(
            out_buf.at[pl.ds(step * heads, heads)],
            out_hbm.at[pl.ds(step * heads, heads)],
            out_sems.at[step],
        )
        for step in range(steps)
    ]
    for step in range(steps):
        for load in loads[step]:
            load.start()
    for step in range(steps):
        for which, load in enumerate(loads[step]):
            load.wait()
            row = which * HEAD_DIM
            for pair in range(step * heads // 2, (step + 1) * heads // 2):
                turned = in_buf[which, :, pair * LANES : (pair + 1) * LANES].T
                out_buf[2 * pair, row : row + HEAD_DIM, :] = turned[:HEAD_DIM]
                out_buf[2 * pair + 1, row : row + HEAD_DIM, :] = turned[HEAD_DIM:]
        stores[step].start()
    for store in stores:
        store.wait()


def pack(query, key, value):
    tokens, width = query.shape
    heads = width // HEAD_DIM
    steps = 4
    hbm = pl.BlockSpec(memory_space=pltpu.HBM)
    return pl.pallas_call(
        pack_kernel,
        out_shape=jax.ShapeDtypeStruct((heads, 3 * HEAD_DIM, tokens), BF16),
        in_specs=[hbm] * 3,
        out_specs=hbm,
        scratch_shapes=[
            pltpu.VMEM((3, tokens, width), BF16),
            pltpu.VMEM((heads, 3 * HEAD_DIM, tokens), BF16),
            pltpu.SemaphoreType.DMA((steps, 3)),
            pltpu.SemaphoreType.DMA((steps,)),
        ],
        compiler_params=params(56),
        cost_estimate=SMALL,
        name="pack",
    )(query, key, value)


Q_ROWS = 512
K_ROWS = 1024
DEPTH = 2 * HEAD_DIM + 16
V_ROWS = HEAD_DIM + 16


def attend_kernel(qkv_ref, out_ref, key_buf, value_buf):
    slabs = qkv_ref.shape[0]
    length = slabs * LANES
    per_block = Q_ROWS // LANES
    largest = jnp.zeros((1, LANES), F32)
    for slab in range(slabs):
        rows = slice(slab * LANES, (slab + 1) * LANES)
        keys = qkv_ref[slab, HEAD_DIM : 2 * HEAD_DIM, :]
        turned = keys.T
        key_buf[rows, 0:HEAD_DIM] = turned
        key_buf[rows, HEAD_DIM : 2 * HEAD_DIM] = turned
        wide = keys.astype(F32)
        largest = jnp.maximum(largest, jnp.sum(wide * wide, axis=0, keepdims=True))
        value_buf[0:HEAD_DIM, rows] = qkv_ref[slab, 2 * HEAD_DIM : 3 * HEAD_DIM, :]
    key_buf[:, 2 * HEAD_DIM : DEPTH] = jnp.ones((length, DEPTH - 2 * HEAD_DIM), BF16)
    value_buf[HEAD_DIM:V_ROWS, :] = jnp.ones((V_ROWS - HEAD_DIM, length), BF16)
    key_bound = jnp.max(largest, axis=1, keepdims=True)

    def load_queries(block):
        return jnp.concatenate(
            [qkv_ref[block * per_block + j, 0:HEAD_DIM, :] for j in range(per_block)], axis=1
        )

    def store(block, total):
        result = (total[0:HEAD_DIM] / total[HEAD_DIM : HEAD_DIM + 1]).astype(BF16)
        for j in range(per_block):
            out_ref[block * per_block + j] = result[:, j * LANES : (j + 1) * LANES]

    first_row = lax.broadcasted_iota(jnp.int32, (DEPTH - 2 * HEAD_DIM, Q_ROWS), 0) == 0

    def step(block, least):
        queries = load_queries(block).astype(F32)
        bound = SCORE_SCALE * jnp.sqrt(
            jnp.sum(queries * queries, axis=0, keepdims=True) * key_bound
        )
        scaled = queries * SCORE_SCALE
        high = scaled.astype(BF16)
        low = (scaled - high.astype(F32)).astype(BF16)
        shift = jnp.where(first_row, -bound, 0.0).astype(BF16)
        stacked = jnp.concatenate([high, low, shift], axis=0)
        total = jnp.zeros((V_ROWS, Q_ROWS), F32)
        for part in range(length // K_ROWS):
            span = slice(part * K_ROWS, (part + 1) * K_ROWS)
            scores = jnp.dot(key_buf[span, :], stacked, preferred_element_type=F32)
            weights = jnp.exp2(scores).astype(BF16)
            total = total + jnp.dot(value_buf[:, span], weights, preferred_element_type=F32)
        store(block, total)
        return jnp.minimum(least, total[HEAD_DIM : HEAD_DIM + 1])

    least = lax.fori_loop(0, length // Q_ROWS, step, jnp.full((1, Q_ROWS), 1.0, F32))

    @pl.when(jnp.min(least) < SMALLEST_SUM)
    def _():
        def careful(block, _):
            queries = load_queries(block)

            def inner(part, state):
                top, total = state
                begin = pl.multiple_of(part * K_ROWS, K_ROWS)
                keys = key_buf[pl.ds(begin, K_ROWS), 0:HEAD_DIM]
                scores = jnp.dot(keys, queries, preferred_element_type=F32)
                higher = jnp.maximum(top, jnp.max(scores, axis=0, keepdims=True))
                weights = jnp.exp2((scores - higher) * SCORE_SCALE).astype(BF16)
                fade = jnp.exp2((top - higher) * SCORE_SCALE)
                added = jnp.dot(
                    value_buf[:, pl.ds(begin, K_ROWS)], weights, preferred_element_type=F32
                )
                return higher, total * fade + added

            start = (jnp.full((1, Q_ROWS), -1e30, F32), jnp.zeros((V_ROWS, Q_ROWS), F32))
            _, total = lax.fori_loop(0, length // K_ROWS, inner, start)
            store(block, total)
            return 0

        lax.fori_loop(0, length // Q_ROWS, careful, 0)


def attend(qkv):
    slabs = qkv.shape[0]
    length = slabs * LANES
    return pl.pallas_call(
        attend_kernel,
        out_shape=jax.ShapeDtypeStruct((slabs, HEAD_DIM, LANES), BF16),
        in_specs=[vmem_spec()],
        out_specs=vmem_spec(),
        scratch_shapes=[pltpu.VMEM((length, DEPTH), BF16), pltpu.VMEM((V_ROWS, length), BF16)],
        compiler_params=params(20),
        cost_estimate=SMALL,
        name="attend",
    )(qkv)


def stage(sources, buffers, sems):
    copies = [
        pltpu.make_async_copy(source, buffer, sems.at[i])
        for i, (source, buffer) in enumerate(zip(sources, buffers))
    ]
    for copy in copies:
        copy.start()
    return copies


def hidden_kernel(pieces, y_ref, *refs):
    arrays = sum(count for _, count in pieces)
    clips = len(pieces)
    parts, refs = refs[:arrays], refs[arrays:]
    residual, out_hbm, first_hbm = refs[:3]
    near = () if clips > 1 else refs[3:4]
    refs = refs[3 + len(near) :]
    hidden_ref, *terms = refs[: 1 + clips]
    rows_buf, residual_buf, out_buf, first_buf, hidden_buf, sems = refs[1 + clips :]
    inner = out_buf.shape[0]
    chunks = 4
    depth = inner // chunks
    span = first_buf.shape[0] // 2
    sources = list(parts) + [residual]
    buffers = []
    for clip, (_, count) in enumerate(pieces):
        size = inner // count
        buffers += [rows_buf.at[clip, pl.ds(k * size, size)] for k in range(count)]
    buffers.append(residual_buf)
    for k in range(chunks):
        sources.append(out_hbm.at[pl.ds(k * depth, depth)])
        buffers.append(out_buf.at[pl.ds(k * depth, depth)])
    for k in range(2):
        sources.append(first_hbm.at[pl.ds(k * span, span)])
        buffers.append(first_buf.at[pl.ds(k * span, span)])
    if near:
        sources += [near[0].at[pl.ds(0, 2)], near[0].at[2]]
        buffers += [hidden_buf.at[pl.ds(0, 2)], hidden_buf.at[3]]
    copies = stage(sources, buffers, sems)
    for copy in copies[: arrays + 1]:
        copy.wait()
    tokens = rows_buf.shape[2]
    mixed = jnp.concatenate(
        [residual_buf[lax.rem(y_ref[0] + r, NY)].astype(F32) for r, _ in pieces], axis=0
    )
    for k in range(chunks):
        part = slice(k * depth, (k + 1) * depth)
        rows = jnp.concatenate([rows_buf[clip, part, :].T for clip in range(clips)], axis=0)
        copies[arrays + 1 + k].wait()
        mixed = mixed + jnp.dot(rows, out_buf[part, :], preferred_element_type=F32)
    hidden = mixed.astype(BF16)
    for clip in range(clips):
        hidden_buf[2 if near else clip] = hidden[clip * tokens : (clip + 1) * tokens]
    for copy in copies[arrays + 1 + chunks :]:
        copy.wait()
    last = pltpu.make_async_copy(hidden_buf, hidden_ref, sems.at[len(sources)])
    last.start()
    for clip, ref in enumerate(terms):
        rows = hidden[clip * tokens : (clip + 1) * tokens]
        ref[...] = jnp.dot(rows, first_buf[...], preferred_element_type=F32).astype(BF16)
    last.wait()


def hidden_rows(pieces, y, parts, residual, out_wide, first_wide, *near):
    inner = out_wide.shape[0]
    tokens = parts[0].shape[1]
    width, hid = first_wide.shape
    clips = len(pieces)
    return pl.pallas_call(
        functools.partial(hidden_kernel, pieces),
        out_shape=(
            jax.ShapeDtypeStruct((NY if near else clips, tokens, width), BF16),
            *[jax.ShapeDtypeStruct((tokens, hid), BF16)] * clips,
        ),
        in_specs=[pl.BlockSpec(memory_space=pltpu.SMEM)]
        + [pl.BlockSpec(memory_space=pl.ANY)] * (3 + len(parts) + len(near)),
        out_specs=(pl.BlockSpec(memory_space=pl.ANY), *[vmem_spec()] * clips),
        scratch_shapes=[
            pltpu.VMEM((clips, inner, tokens), BF16),
            pltpu.VMEM((NY, tokens, width), BF16),
            pltpu.VMEM((inner, width), BF16),
            pltpu.VMEM((width, hid), BF16),
            pltpu.VMEM((NY if near else clips, tokens, width), BF16),
            pltpu.SemaphoreType.DMA((len(parts) + 8 + 2 * len(near),)),
        ],
        compiler_params=params(56),
        cost_estimate=SMALL,
        name="hidden",
    )(y.reshape(1), *parts, residual, out_wide, first_wide, *near)


def similar_kernel(
    place_ref, own_hbm, one_hbm, two_hbm, three_hbm, target_hbm, own_0, own_1, own_3, own_2, own_2b,
    peer_0, peer_1, peer_3, peer_2, peer_2b, first_bias_ref, second_bias_ref, send_0, send_1, send_2, send_3, pre_grad_ref, cosine_ref,
    terms_ref, target_ref, second_ref, active_ref, slope_ref, sems,
):
    hid, outf = second_ref.shape
    depth = own_0.shape[0]
    sources = [own_hbm, one_hbm, two_hbm, three_hbm]
    buffers = [terms_ref.at[r] for r in range(NY)]
    spans = []
    for parity, second in (
        (place_ref[1], (own_0, own_1, own_3, own_2, own_2b)),
        (1 - place_ref[1], (peer_0, peer_1, peer_3, peer_2, peer_2b)),
    ):
        for piece, r in zip(second, (0, 1, 3, 2, 2)):
            rows = piece.shape[0]
            owner = 2 * lax.rem(place_ref[0] + r, NY) + parity
            begin = owner * depth + (rows if piece is second[-1] else 0)
            spans.append(pl.ds(pl.multiple_of(begin, rows), rows))
            sources.append(piece)
            buffers.append(second_ref.at[spans[-1]])
    copies = stage(sources + [target_hbm], buffers + [target_ref], sems)
    for copy in copies[:NY]:
        copy.wait()
    preact = first_bias_ref[...] + sum(terms_ref[r].astype(F32) for r in range(NY))
    gate = 1.0 / (1.0 + jnp.exp(-preact))
    active_ref[...] = (preact * gate).astype(BF16)
    slope_ref[...] = gate * (1.0 + preact * (1.0 - gate))
    projected = jnp.broadcast_to(second_bias_ref[...], target_ref.shape)
    for k, span in enumerate(spans):
        copies[NY + k].wait()
        projected = projected + jnp.dot(
            active_ref[:, span], second_ref[span, :], preferred_element_type=F32
        )
    copies[-1].wait()
    target = target_ref[...]
    inv_model = lax.rsqrt(jnp.sum(projected * projected, axis=1, keepdims=True) + EPSILON)
    inv_target = lax.rsqrt(jnp.sum(target * target, axis=1, keepdims=True) + EPSILON)
    cosine = jnp.sum(projected * target, axis=1, keepdims=True) * inv_model * inv_target
    cosine_ref[...] = cosine
    row_grad = (
        -math.sqrt(outf) * inv_model * (target * inv_target - cosine * inv_model * projected)
    ).astype(BF16)
    units = hid // NY
    for r, send in enumerate((send_0, send_1, send_2, send_3)):
        chip = lax.rem(place_ref[0] + (NY - r), NY)
        send[:, :units] = active_ref[:, pl.ds(pl.multiple_of(chip * units, units), units)]
        send[:, units:] = row_grad
    cols = hid // NX
    for quarter in range(NX):
        span = slice(quarter * cols, (quarter + 1) * cols)
        back = lax.dot_general(
            row_grad, second_ref[span, :], (((1,), (1,)), ((), ())), preferred_element_type=F32
        )
        pre_grad_ref[quarter] = (back * slope_ref[:, span]).astype(BF16)


def similar(place, terms, first_bias, seconds, second_bias, target):
    tokens, hid = terms[0].shape
    outf = seconds[0].shape[1]
    send = jax.ShapeDtypeStruct((tokens, hid // NY + outf), BF16)
    specs = [pl.BlockSpec(memory_space=pl.ANY)] * (NY + 1 + len(seconds)) + [vmem_spec()] * 2
    return pl.pallas_call(
        similar_kernel,
        out_shape=(
            (send,) * NY
            + (
                jax.ShapeDtypeStruct((NX, tokens, hid // NX), BF16),
                jax.ShapeDtypeStruct((tokens, 1), F32),
            )
        ),
        in_specs=[pl.BlockSpec(memory_space=pltpu.SMEM)] + specs,
        out_specs=(vmem_spec(),) * (NY + 2),
        scratch_shapes=[
            pltpu.VMEM((NY, tokens, hid), BF16),
            pltpu.VMEM((tokens, outf), F32),
            pltpu.VMEM((hid, outf), BF16),
            pltpu.VMEM((tokens, hid), BF16),
            pltpu.VMEM((tokens, hid), F32),
            pltpu.SemaphoreType.DMA((NY + 1 + len(seconds),)),
        ],
        compiler_params=params(56),
        cost_estimate=SMALL,
        name="similar",
    )(
        place, *terms, target, *seconds, first_bias.reshape(1, -1),
        second_bias.reshape(1, -1),
    )


def second_kernel(core_ref, one, two, three, four, keep_ref, give_ref):
    units = 2 * keep_ref.shape[1]
    cols = keep_ref.shape[2]
    parts = (one, two, three, four)
    active = jnp.concatenate([part[:, :units] for part in parts], axis=0).T
    grads = [
        jnp.concatenate(
            [part[:, units + x * cols : units + (x + 1) * cols] for part in parts], axis=0
        )
        for x in range(NX)
    ]
    half = units // 2
    for x in range(NX):
        total = jnp.dot(active, grads[x], preferred_element_type=F32).astype(BF16)
        top, bottom = total[:half], total[half:]
        first = core_ref[0] == 0
        keep_ref[x] = jnp.where(first, top, bottom)
        give_ref[x] = jnp.where(first, bottom, top)


def second_gradient(core, parts, units, outf):
    shape = jax.ShapeDtypeStruct((NX, units, outf // NX), BF16)
    return pl.pallas_call(
        second_kernel,
        out_shape=(shape, shape),
        in_specs=[pl.BlockSpec(memory_space=pltpu.SMEM)] + [vmem_spec()] * NY,
        out_specs=(vmem_spec(), vmem_spec()),
        compiler_params=params(24),
        cost_estimate=LARGE,
        name="second",
    )(core.reshape(1), *parts)


def first_kernel(clips, x_ref, *refs):
    hidden_own, hidden_up, hidden_down, hidden_top, hidden_bottom = refs[:5]
    refs = refs[5:]
    arrays = sum(count for _, count in clips)
    parts, refs = refs[:arrays], refs[arrays:]
    last = len(clips) == 1
    if last:
        before, keep_ref, give_ref, hidden_buf, grad_buf, total_buf, sems = refs
    else:
        total_ref, hidden_buf, grad_buf, sems = refs
    sources = []
    buffers = []
    half = NY // 2
    for i, (r, count) in enumerate(clips):
        across = hidden_top.at[r] if r < half else hidden_bottom.at[r - half]
        for d, source in enumerate((hidden_own.at[r], hidden_up.at[r], across, hidden_down.at[r])):
            sources.append(source)
            buffers.append(hidden_buf.at[i, lax.rem(x_ref[0] + d, NX)])
        size = NX // count
        buffers += [grad_buf.at[i, pl.ds(k * size, size)] for k in range(count)]
        sources += parts[:count]
        parts = parts[count:]
    if last:
        sources.append(before)
        buffers.append(total_buf)
    copies = stage(sources, buffers, sems)
    total = 0.0
    for i, (_, count) in enumerate(clips):
        for copy in copies[: count + NX]:
            copy.wait()
        copies = copies[count + NX :]
        left = hidden_buf[i].reshape(-1, hidden_buf.shape[3])
        right = grad_buf[i].reshape(-1, grad_buf.shape[3])
        total = total + jnp.dot(left.T, right, preferred_element_type=F32)
    if last:
        width = keep_ref.shape[0]
        copies[0].wait()
        total = total + total_buf[...]
        keep_ref[...] = total[:width].astype(BF16)
        give_ref[...] = total[width:].astype(BF16)
    else:
        total_ref[...] = total


def first_gradient(clips, x, hidden, grads, *before):
    _, tokens, width = hidden[0].shape
    cols = grads[0].shape[2]
    if before:
        out_shape = (jax.ShapeDtypeStruct((width // 2, cols), BF16),) * 2
    else:
        out_shape = jax.ShapeDtypeStruct((width, cols), F32)
    return pl.pallas_call(
        functools.partial(first_kernel, clips),
        out_shape=out_shape,
        in_specs=[pl.BlockSpec(memory_space=pltpu.SMEM)]
        + [pl.BlockSpec(memory_space=pl.ANY)] * (len(hidden) + len(grads) + len(before)),
        out_specs=(vmem_spec(), vmem_spec()) if before else vmem_spec(),
        scratch_shapes=[
            pltpu.VMEM((len(clips), NX, tokens, width), BF16),
            pltpu.VMEM((len(clips), NX, tokens, cols), BF16),
            *[pltpu.VMEM(total.shape, F32) for total in before],
            pltpu.SemaphoreType.DMA((NX * len(clips) + len(grads) + len(before),)),
        ],
        compiler_params=params(56),
        cost_estimate=SMALL,
        name="first",
    )(x.reshape(1), *hidden, *grads, *before)


def arrange_kernel(own_ref, other_ref, second_ref, out_ref):
    first = own_ref[...].astype(F32) + other_ref[...].astype(F32)
    second = second_ref[0].astype(F32)
    for x in range(1, NX):
        second = second + second_ref[x].astype(F32)
    for z in range(NZ):
        row = 0
        for total in (first.astype(BF16), second.astype(BF16)):
            rows = total.shape[0] // NZ
            for lane in range(total.shape[1] // LANES):
                out_ref[z // 2, z % 2, row : row + rows, :] = total[
                    z * rows : (z + 1) * rows, lane * LANES : (lane + 1) * LANES
                ]
                row += rows


def arrange(own, other, second):
    rows = (own.size + second[0].size) // (NZ * LANES)
    return pl.pallas_call(
        arrange_kernel,
        out_shape=jax.ShapeDtypeStruct((NZ // 2, 2, rows, LANES), BF16),
        in_specs=[vmem_spec()] * 3,
        out_specs=vmem_spec(),
        compiler_params=params(16),
        cost_estimate=SMALL,
        name="arrange",
    )(own, other, second)


def part_kernel(parity_ref, blocks_ref, keep_ref, give_ref):
    for index, ref in ((parity_ref[0], keep_ref), (1 - parity_ref[0], give_ref)):
        total = blocks_ref[0, index].astype(F32)
        for pair in range(1, NZ // 2):
            total = total + blocks_ref[pair, index].astype(F32)
        ref[...] = total.astype(ref.dtype)


def part(parity, blocks):
    return pl.pallas_call(
        part_kernel,
        out_shape=(
            jax.ShapeDtypeStruct(blocks.shape[2:], F32),
            jax.ShapeDtypeStruct(blocks.shape[2:], BF16),
        ),
        in_specs=[pl.BlockSpec(memory_space=pltpu.SMEM), vmem_spec()],
        out_specs=(vmem_spec(), vmem_spec()),
        compiler_params=params(16),
        cost_estimate=SMALL,
        name="part",
    )(parity.reshape(1), blocks)


def unpack_kernel(place_ref, *refs):
    *parts, first_ref, second_ref = refs
    for index, part in enumerate(parts):
        column = lax.rem(place_ref[0] + index // 2, NX)
        parity = lax.rem(place_ref[1] + index % 2, 2)
        for pair in range(NZ // 2):
            z = 2 * pair + parity
            row = 0
            for ref in (first_ref, second_ref):
                rows = ref.shape[0] // NZ
                cols = ref.shape[1] // NX
                to_row = pl.multiple_of(z * rows, rows)
                for lane in range(cols // LANES):
                    to_lane = pl.multiple_of(column * cols + lane * LANES, LANES)
                    ref[pl.ds(to_row, rows), pl.ds(to_lane, LANES)] = part[
                        pair, row : row + rows, :
                    ]
                    row += rows


def unpack(place, parts, first_shape, second_shape):
    return pl.pallas_call(
        unpack_kernel,
        out_shape=(
            jax.ShapeDtypeStruct(first_shape, BF16),
            jax.ShapeDtypeStruct(second_shape, BF16),
        ),
        in_specs=[pl.BlockSpec(memory_space=pltpu.SMEM)] + [vmem_spec()] * len(parts),
        out_specs=(vmem_spec(), vmem_spec()),
        compiler_params=params(16),
        cost_estimate=SMALL,
        name="unpack",
    )(place, *parts)


def after(values, *others):
    return lax.optimization_barrier((values, others))[0]


def body(
    query_in,
    key_in,
    value_in,
    residual,
    out_proj,
    first_proj,
    first_bias,
    second_proj,
    second_bias,
    teacher,
    teach_index,
    teach_weight,
):
    dp = lax.axis_index("dp")
    seq = lax.axis_index("seq")
    y, core = dp // 2, lax.rem(dp, 2)
    x = seq // NZ
    tokens = query_in.shape[1]
    width = residual.shape[2]
    hid = first_bias.shape[0]
    outf = second_bias.shape[0]

    swap = functools.partial(lax.ppermute, axis_name="dp", perm=core_swap())

    def from_y(value, by):
        return lax.ppermute(value, "dp", dp_shift(-by))

    seconds = [second_proj, from_y(second_proj, 1), from_y(second_proj, 3)]
    middle = second_proj.shape[0] // 2
    seconds += [from_y(seconds[1][:middle], 1), from_y(seconds[2][middle:], 3)]
    peers = [swap(second_proj)]
    out_wide = jnp.concatenate([out_proj, swap(out_proj)], axis=1)
    first_wide = jnp.concatenate([first_proj, swap(first_proj)], axis=0)
    by_core = residual.reshape(NY, 2, tokens, width)
    mine = lax.dynamic_index_in_dim(by_core, core, 1, keepdims=False)
    theirs = lax.dynamic_index_in_dim(by_core, 1 - core, 1, keepdims=False)
    residual_wide = jnp.concatenate([mine, swap(theirs)], axis=2)

    local = teacher[0]
    rows = local.shape[0]
    count = lax.axis_size("seq")
    earlier = lax.ppermute(local, "seq", [(i, i + 1) for i in range(count - 1)])
    later = lax.ppermute(local, "seq", [(i + 1, i) for i in range(count - 1)])
    window = jnp.concatenate([earlier, local, later], axis=0)
    offsets = teach_index - (seq - 1) * rows
    spots = jnp.arange(3 * rows, dtype=jnp.int32)
    blend = jnp.sum(
        jnp.where(offsets[:, :, None] == spots, teach_weight[:, :, None], 0.0), axis=1
    )
    target = jnp.dot(blend, window.astype(F32), precision=lax.Precision.HIGHEST)

    qkv = lax.all_to_all(
        pack(query_in[0], key_in[0], value_in[0]), "seq", 0, 0, tiled=True
    )
    qkv = after(qkv, out_wide, first_wide, residual_wide, seconds, peers[0])
    attended = lax.all_to_all(attend(qkv), "seq", 0, 0, tiled=True)
    peers += [swap(second) for second in seconds[1:]]
    attended = after(attended.reshape(-1, tokens), target, peers)

    def from_x(value, by):
        return lax.ppermute(value, "seq", x_shift(-by))

    half = attended.shape[0] // 2
    upper = from_y(attended, 1)
    lower = from_y(attended, 3)
    across = [from_y(upper[:half], 1), from_y(lower[half:], 3)]
    near, *near_terms = hidden_rows(
        ((0, 1), (1, 1), (3, 1)), y, [attended, upper, lower], residual_wide, out_wide, first_wide
    )
    across = after(across, near)
    hidden, far_term = hidden_rows(
        ((2, 2),), y, across, residual_wide, out_wide, first_wide, near
    )
    terms = [
        near_terms[0],
        lax.ppermute(near_terms[1], "dp", dp_shift(1)),
        lax.ppermute(far_term, "dp", dp_shift(2)),
        lax.ppermute(near_terms[2], "dp", dp_shift(3)),
    ]

    hidden_up = from_x(hidden, 1)
    hidden_down = from_x(hidden, 3)
    terms = after(terms, hidden_up, hidden_down)
    hidden_x = [
        hidden,
        hidden_up,
        hidden_down,
        from_x(hidden_up[: NY // 2], 1),
        from_x(hidden_down[NY // 2 :], 3),
    ]

    *sends, pre_grad, cosine = similar(
        jnp.stack([y, core]), terms, first_bias, seconds + peers, second_bias, target
    )
    pre_grad = after(pre_grad, hidden_x)
    sends = [sends[0]] + [from_y(sends[r], r) for r in range(1, NY)]

    pre_x = lax.all_to_all(pre_grad, "seq", 0, 0, tiled=True, axis_index_groups=X_GROUPS)
    upper = from_y(pre_x, 1)
    lower = from_y(pre_x, 3)
    across = [from_y(upper[: NX // 2], 1), from_y(lower[NX // 2 :], 3)]

    units = second_proj.shape[0]
    keep, give = second_gradient(core, after(sends, pre_x), units, outf)
    second_own = (keep.astype(F32) + swap(give).astype(F32)).astype(BF16)
    second_parts = lax.all_to_all(
        second_own, "seq", 0, 0, tiled=True, axis_index_groups=X_GROUPS
    )
    total = first_gradient(((1, 1), (3, 1), (0, 1)), x, hidden_x, [upper, lower, pre_x])
    across = after(across, total)
    first_own, first_give = first_gradient(((2, 2),), x, hidden_x, across, total)

    z = lax.rem(seq, NZ)
    blocks = arrange(first_own, swap(first_give), second_parts)
    blocks = lax.all_to_all(blocks, "seq", 0, 0, tiled=True, axis_index_groups=PARITY_GROUPS)
    keep, give = part(lax.rem(z, 2), blocks)
    summed = (keep + lax.ppermute(give, "seq", z_swap()).astype(F32)).astype(BF16)

    same = lax.all_gather(summed, "seq", axis=0, axis_index_groups=PARITY_GROUPS)
    other = lax.ppermute(same, "seq", z_swap())
    same_x = {0: same, 1: from_x(same, 1), 3: from_x(same, 3)}
    other_x = {0: other, 1: from_x(other, 1), 3: from_x(other, 3)}
    same_x[2] = from_x(same_x[1], 1)
    other_x[2] = from_x(other_x[3], 3)
    grad_first, grad_second = unpack(
        jnp.stack([x, z]),
        [part for d in range(NX) for part in (same_x[d], other_x[d])],
        (width, hid),
        (units, outf),
    )
    return (cosine.reshape(1, -1), grad_first, grad_second)


def solution(mesh):
    placed = (
        P("dp", "seq", None),
        P("dp", "seq", None),
        P("dp", "seq", None),
        P(None, "seq", "dp"),
        P(None, "dp"),
        P("dp", None),
        P(),
        P("dp", None),
        P(),
        P("dp", "seq", None),
        P("seq", None),
        P("seq", None),
    )
    return jax.shard_map(
        body,
        mesh=mesh,
        in_specs=placed,
        out_specs=(P("dp", "seq"), P("dp", None), P("dp", None)),
        check_vma=False,
    )
```

```python
import functools
import math

import jax
import jax.numpy as jnp
from jax import lax
from jax.experimental import pallas as pl
from jax.experimental.pallas import tpu as pltpu
from jax.sharding import PartitionSpec as P

HEAD_DIM = 64
LANES = 128
EPSILON = 1e-06
SCORE_SCALE = HEAD_DIM ** (-0.5) * math.log2(math.e)
SMALLEST_SUM = 2.0 ** -90
BF16 = jnp.bfloat16
F32 = jnp.float32
NX, NZ, NY = 4, 8, 4
LARGE = pl.CostEstimate(flops=2**35, bytes_accessed=2**23, transcendentals=0)
SMALL = pl.CostEstimate(flops=0, bytes_accessed=0, transcendentals=0)


def dp_shift(by):
    return [(i, (i + 2 * by) % (2 * NY)) for i in range(2 * NY)]


def core_swap():
    return [(i, i ^ 1) for i in range(2 * NY)]


def x_shift(by):
    return [(x * NZ + z, ((x + by) % NX) * NZ + z) for x in range(NX) for z in range(NZ)]


def z_swap():
    return [(i, i ^ 1) for i in range(NX * NZ)]


X_GROUPS = [[x * NZ + z for x in range(NX)] for z in range(NZ)]
PARITY_GROUPS = [
    [x * NZ + 2 * pair + parity for pair in range(NZ // 2)]
    for x in range(NX)
    for parity in range(2)
]


def vmem_spec():
    return pl.BlockSpec(memory_space=pltpu.VMEM)


def params(mib):
    return pltpu.CompilerParams(vmem_limit_bytes=mib * 1024 * 1024)


def pack_kernel(query_hbm, key_hbm, value_hbm, out_hbm, in_buf, out_buf, in_sems, out_sems):
    steps = in_sems.shape[0]
    cols = in_buf.shape[2] // steps
    heads = out_buf.shape[0] // steps
    loads = [
        [
            pltpu.make_async_copy(
                source.at[:, pl.ds(step * cols, cols)],
                in_buf.at[which, :, pl.ds(step * cols, cols)],
                in_sems.at[step, which],
            )
            for which, source in enumerate((query_hbm, key_hbm, value_hbm))
        ]
        for step in range(steps)
    ]
    stores = [
        pltpu.make_async_copy(
            out_buf.at[pl.ds(step * heads, heads)],
            out_hbm.at[pl.ds(step * heads, heads)],
            out_sems.at[step],
        )
        for step in range(steps)
    ]
    for step in range(steps):
        for load in loads[step]:
            load.start()
    for step in range(steps):
        for which, load in enumerate(loads[step]):
            load.wait()
            row = which * HEAD_DIM
            for pair in range(step * heads // 2, (step + 1) * heads // 2):
                turned = in_buf[which, :, pair * LANES : (pair + 1) * LANES].T
                out_buf[2 * pair, row : row + HEAD_DIM, :] = turned[:HEAD_DIM]
                out_buf[2 * pair + 1, row : row + HEAD_DIM, :] = turned[HEAD_DIM:]
        stores[step].start()
    for store in stores:
        store.wait()


def pack(query, key, value):
    tokens, width = query.shape
    heads = width // HEAD_DIM
    steps = 4
    hbm = pl.BlockSpec(memory_space=pltpu.HBM)
    return pl.pallas_call(
        pack_kernel,
        out_shape=jax.ShapeDtypeStruct((heads, 3 * HEAD_DIM, tokens), BF16),
        in_specs=[hbm] * 3,
        out_specs=hbm,
        scratch_shapes=[
            pltpu.VMEM((3, tokens, width), BF16),
            pltpu.VMEM((heads, 3 * HEAD_DIM, tokens), BF16),
            pltpu.SemaphoreType.DMA((steps, 3)),
            pltpu.SemaphoreType.DMA((steps,)),
        ],
        compiler_params=params(56),
        cost_estimate=SMALL,
        name="pack",
    )(query, key, value)


Q_ROWS = 512
K_ROWS = 1024
DEPTH = 2 * HEAD_DIM + 16
V_ROWS = HEAD_DIM + 16


def attend_kernel(qkv_ref, out_ref, key_buf, value_buf):
    slabs = qkv_ref.shape[0]
    length = slabs * LANES
    per_block = Q_ROWS // LANES
    largest = jnp.zeros((1, LANES), F32)
    for slab in range(slabs):
        rows = slice(slab * LANES, (slab + 1) * LANES)
        keys = qkv_ref[slab, HEAD_DIM : 2 * HEAD_DIM, :]
        turned = keys.T
        key_buf[rows, 0:HEAD_DIM] = turned
        key_buf[rows, HEAD_DIM : 2 * HEAD_DIM] = turned
        wide = keys.astype(F32)
        largest = jnp.maximum(largest, jnp.sum(wide * wide, axis=0, keepdims=True))
        value_buf[0:HEAD_DIM, rows] = qkv_ref[slab, 2 * HEAD_DIM : 3 * HEAD_DIM, :]
    key_buf[:, 2 * HEAD_DIM : DEPTH] = jnp.ones((length, DEPTH - 2 * HEAD_DIM), BF16)
    value_buf[HEAD_DIM:V_ROWS, :] = jnp.ones((V_ROWS - HEAD_DIM, length), BF16)
    key_bound = jnp.max(largest, axis=1, keepdims=True)

    def load_queries(block):
        return jnp.concatenate(
            [qkv_ref[block * per_block + j, 0:HEAD_DIM, :] for j in range(per_block)], axis=1
        )

    def store(block, total):
        result = (total[0:HEAD_DIM] / total[HEAD_DIM : HEAD_DIM + 1]).astype(BF16)
        for j in range(per_block):
            out_ref[block * per_block + j] = result[:, j * LANES : (j + 1) * LANES]

    first_row = lax.broadcasted_iota(jnp.int32, (DEPTH - 2 * HEAD_DIM, Q_ROWS), 0) == 0

    def step(block, least):
        queries = load_queries(block).astype(F32)
        bound = SCORE_SCALE * jnp.sqrt(
            jnp.sum(queries * queries, axis=0, keepdims=True) * key_bound
        )
        scaled = queries * SCORE_SCALE
        high = scaled.astype(BF16)
        low = (scaled - high.astype(F32)).astype(BF16)
        shift = jnp.where(first_row, -bound, 0.0).astype(BF16)
        stacked = jnp.concatenate([high, low, shift], axis=0)
        total = jnp.zeros((V_ROWS, Q_ROWS), F32)
        for part in range(length // K_ROWS):
            span = slice(part * K_ROWS, (part + 1) * K_ROWS)
            scores = jnp.dot(key_buf[span, :], stacked, preferred_element_type=F32)
            weights = jnp.exp2(scores).astype(BF16)
            total = total + jnp.dot(value_buf[:, span], weights, preferred_element_type=F32)
        store(block, total)
        return jnp.minimum(least, total[HEAD_DIM : HEAD_DIM + 1])

    least = lax.fori_loop(0, length // Q_ROWS, step, jnp.full((1, Q_ROWS), 1.0, F32))

    @pl.when(jnp.min(least) < SMALLEST_SUM)
    def _():
        def careful(block, _):
            queries = load_queries(block)

            def inner(part, state):
                top, total = state
                begin = pl.multiple_of(part * K_ROWS, K_ROWS)
                keys = key_buf[pl.ds(begin, K_ROWS), 0:HEAD_DIM]
                scores = jnp.dot(keys, queries, preferred_element_type=F32)
                higher = jnp.maximum(top, jnp.max(scores, axis=0, keepdims=True))
                weights = jnp.exp2((scores - higher) * SCORE_SCALE).astype(BF16)
                fade = jnp.exp2((top - higher) * SCORE_SCALE)
                added = jnp.dot(
                    value_buf[:, pl.ds(begin, K_ROWS)], weights, preferred_element_type=F32
                )
                return higher, total * fade + added

            start = (jnp.full((1, Q_ROWS), -1e30, F32), jnp.zeros((V_ROWS, Q_ROWS), F32))
            _, total = lax.fori_loop(0, length // K_ROWS, inner, start)
            store(block, total)
            return 0

        lax.fori_loop(0, length // Q_ROWS, careful, 0)


def attend(qkv):
    slabs = qkv.shape[0]
    length = slabs * LANES
    return pl.pallas_call(
        attend_kernel,
        out_shape=jax.ShapeDtypeStruct((slabs, HEAD_DIM, LANES), BF16),
        in_specs=[vmem_spec()],
        out_specs=vmem_spec(),
        scratch_shapes=[pltpu.VMEM((length, DEPTH), BF16), pltpu.VMEM((V_ROWS, length), BF16)],
        compiler_params=params(20),
        cost_estimate=SMALL,
        name="attend",
    )(qkv)


def stage(sources, buffers, sems):
    copies = [
        pltpu.make_async_copy(source, buffer, sems.at[i])
        for i, (source, buffer) in enumerate(zip(sources, buffers))
    ]
    for copy in copies:
        copy.start()
    return copies


def hidden_kernel(pieces, y_ref, *refs):
    arrays = sum(count for _, count in pieces)
    clips = len(pieces)
    parts, refs = refs[:arrays], refs[arrays:]
    residual, out_hbm, first_hbm = refs[:3]
    near = () if clips > 1 else refs[3:4]
    refs = refs[3 + len(near) :]
    hidden_ref, *terms = refs[: 1 + clips]
    rows_buf, residual_buf, out_buf, first_buf, hidden_buf, sems = refs[1 + clips :]
    inner = out_buf.shape[0]
    chunks = 4
    depth = inner // chunks
    span = first_buf.shape[0] // 2
    sources = list(parts) + [residual]
    buffers = []
    for clip, (_, count) in enumerate(pieces):
        size = inner // count
        buffers += [rows_buf.at[clip, pl.ds(k * size, size)] for k in range(count)]
    buffers.append(residual_buf)
    for k in range(chunks):
        sources.append(out_hbm.at[pl.ds(k * depth, depth)])
        buffers.append(out_buf.at[pl.ds(k * depth, depth)])
    for k in range(2):
        sources.append(first_hbm.at[pl.ds(k * span, span)])
        buffers.append(first_buf.at[pl.ds(k * span, span)])
    if near:
        sources += [near[0].at[pl.ds(0, 2)], near[0].at[2]]
        buffers += [hidden_buf.at[pl.ds(0, 2)], hidden_buf.at[3]]
    copies = stage(sources, buffers, sems)
    for copy in copies[: arrays + 1]:
        copy.wait()
    tokens = rows_buf.shape[2]
    mixed = jnp.concatenate(
        [residual_buf[lax.rem(y_ref[0] + r, NY)].astype(F32) for r, _ in pieces], axis=0
    )
    for k in range(chunks):
        part = slice(k * depth, (k + 1) * depth)
        rows = jnp.concatenate([rows_buf[clip, part, :].T for clip in range(clips)], axis=0)
        copies[arrays + 1 + k].wait()
        mixed = mixed + jnp.dot(rows, out_buf[part, :], preferred_element_type=F32)
    hidden = mixed.astype(BF16)
    for clip in range(clips):
        hidden_buf[2 if near else clip] = hidden[clip * tokens : (clip + 1) * tokens]
    for copy in copies[arrays + 1 + chunks :]:
        copy.wait()
    last = pltpu.make_async_copy(hidden_buf, hidden_ref, sems.at[len(sources)])
    last.start()
    for clip, ref in enumerate(terms):
        rows = hidden[clip * tokens : (clip + 1) * tokens]
        ref[...] = jnp.dot(rows, first_buf[...], preferred_element_type=F32).astype(BF16)
    last.wait()


def hidden_rows(pieces, y, parts, residual, out_wide, first_wide, *near):
    inner = out_wide.shape[0]
    tokens = parts[0].shape[1]
    width, hid = first_wide.shape
    clips = len(pieces)
    return pl.pallas_call(
        functools.partial(hidden_kernel, pieces),
        out_shape=(
            jax.ShapeDtypeStruct((NY if near else clips, tokens, width), BF16),
            *[jax.ShapeDtypeStruct((tokens, hid), BF16)] * clips,
        ),
        in_specs=[pl.BlockSpec(memory_space=pltpu.SMEM)]
        + [pl.BlockSpec(memory_space=pl.ANY)] * (3 + len(parts) + len(near)),
        out_specs=(pl.BlockSpec(memory_space=pl.ANY), *[vmem_spec()] * clips),
        scratch_shapes=[
            pltpu.VMEM((clips, inner, tokens), BF16),
            pltpu.VMEM((NY, tokens, width), BF16),
            pltpu.VMEM((inner, width), BF16),
            pltpu.VMEM((width, hid), BF16),
            pltpu.VMEM((NY if near else clips, tokens, width), BF16),
            pltpu.SemaphoreType.DMA((len(parts) + 8 + 2 * len(near),)),
        ],
        compiler_params=params(56),
        cost_estimate=SMALL,
        name="hidden",
    )(y.reshape(1), *parts, residual, out_wide, first_wide, *near)


def similar_kernel(
    place_ref, own_hbm, one_hbm, two_hbm, three_hbm, target_hbm, own_0, own_1, own_3, own_2, own_2b,
    peer_0, peer_1, peer_3, peer_2, peer_2b, first_bias_ref, second_bias_ref, send_0, send_1, send_2, send_3, pre_grad_ref, cosine_ref,
    terms_ref, target_ref, second_ref, active_ref, slope_ref, sems,
):
    hid, outf = second_ref.shape
    depth = own_0.shape[0]
    sources = [own_hbm, one_hbm, two_hbm, three_hbm]
    buffers = [terms_ref.at[r] for r in range(NY)]
    spans = []
    for parity, second in (
        (place_ref[1], (own_0, own_1, own_3, own_2, own_2b)),
        (1 - place_ref[1], (peer_0, peer_1, peer_3, peer_2, peer_2b)),
    ):
        for piece, r in zip(second, (0, 1, 3, 2, 2)):
            rows = piece.shape[0]
            owner = 2 * lax.rem(place_ref[0] + r, NY) + parity
            begin = owner * depth + (rows if piece is second[-1] else 0)
            spans.append(pl.ds(pl.multiple_of(begin, rows), rows))
            sources.append(piece)
            buffers.append(second_ref.at[spans[-1]])
    copies = stage(sources + [target_hbm], buffers + [target_ref], sems)
    for copy in copies[:NY]:
        copy.wait()
    preact = first_bias_ref[...] + sum(terms_ref[r].astype(F32) for r in range(NY))
    gate = 1.0 / (1.0 + jnp.exp(-preact))
    active_ref[...] = (preact * gate).astype(BF16)
    slope_ref[...] = gate * (1.0 + preact * (1.0 - gate))
    projected = jnp.broadcast_to(second_bias_ref[...], target_ref.shape)
    for k, span in enumerate(spans):
        copies[NY + k].wait()
        projected = projected + jnp.dot(
            active_ref[:, span], second_ref[span, :], preferred_element_type=F32
        )
    copies[-1].wait()
    target = target_ref[...]
    inv_model = lax.rsqrt(jnp.sum(projected * projected, axis=1, keepdims=True) + EPSILON)
    inv_target = lax.rsqrt(jnp.sum(target * target, axis=1, keepdims=True) + EPSILON)
    cosine = jnp.sum(projected * target, axis=1, keepdims=True) * inv_model * inv_target
    cosine_ref[...] = cosine
    row_grad = (
        -math.sqrt(outf) * inv_model * (target * inv_target - cosine * inv_model * projected)
    ).astype(BF16)
    units = hid // NY
    for r, send in enumerate((send_0, send_1, send_2, send_3)):
        chip = lax.rem(place_ref[0] + (NY - r), NY)
        send[:, :units] = active_ref[:, pl.ds(pl.multiple_of(chip * units, units), units)]
        send[:, units:] = row_grad
    cols = hid // NX
    for quarter in range(NX):
        span = slice(quarter * cols, (quarter + 1) * cols)
        back = lax.dot_general(
            row_grad, second_ref[span, :], (((1,), (1,)), ((), ())), preferred_element_type=F32
        )
        pre_grad_ref[quarter] = (back * slope_ref[:, span]).astype(BF16)


def similar(place, terms, first_bias, seconds, second_bias, target):
    tokens, hid = terms[0].shape
    outf = seconds[0].shape[1]
    send = jax.ShapeDtypeStruct((tokens, hid // NY + outf), BF16)
    specs = [pl.BlockSpec(memory_space=pl.ANY)] * (NY + 1 + len(seconds)) + [vmem_spec()] * 2
    return pl.pallas_call(
        similar_kernel,
        out_shape=(
            (send,) * NY
            + (
                jax.ShapeDtypeStruct((NX, tokens, hid // NX), BF16),
                jax.ShapeDtypeStruct((tokens, 1), F32),
            )
        ),
        in_specs=[pl.BlockSpec(memory_space=pltpu.SMEM)] + specs,
        out_specs=(vmem_spec(),) * (NY + 2),
        scratch_shapes=[
            pltpu.VMEM((NY, tokens, hid), BF16),
            pltpu.VMEM((tokens, outf), F32),
            pltpu.VMEM((hid, outf), BF16),
            pltpu.VMEM((tokens, hid), BF16),
            pltpu.VMEM((tokens, hid), F32),
            pltpu.SemaphoreType.DMA((NY + 1 + len(seconds),)),
        ],
        compiler_params=params(56),
        cost_estimate=SMALL,
        name="similar",
    )(
        place, *terms, target, *seconds, first_bias.reshape(1, -1),
        second_bias.reshape(1, -1),
    )


def second_kernel(core_ref, one, two, three, four, keep_ref, give_ref):
    units = 2 * keep_ref.shape[1]
    cols = keep_ref.shape[2]
    parts = (one, two, three, four)
    active = jnp.concatenate([part[:, :units] for part in parts], axis=0).T
    grads = [
        jnp.concatenate(
            [part[:, units + x * cols : units + (x + 1) * cols] for part in parts], axis=0
        )
        for x in range(NX)
    ]
    half = units // 2
    for x in range(NX):
        total = jnp.dot(active, grads[x], preferred_element_type=F32).astype(BF16)
        top, bottom = total[:half], total[half:]
        first = core_ref[0] == 0
        keep_ref[x] = jnp.where(first, top, bottom)
        give_ref[x] = jnp.where(first, bottom, top)


def second_gradient(core, parts, units, outf):
    shape = jax.ShapeDtypeStruct((NX, units, outf // NX), BF16)
    return pl.pallas_call(
        second_kernel,
        out_shape=(shape, shape),
        in_specs=[pl.BlockSpec(memory_space=pltpu.SMEM)] + [vmem_spec()] * NY,
        out_specs=(vmem_spec(), vmem_spec()),
        compiler_params=params(24),
        cost_estimate=LARGE,
        name="second",
    )(core.reshape(1), *parts)


def first_kernel(clips, x_ref, *refs):
    hidden_own, hidden_up, hidden_down, hidden_top, hidden_bottom = refs[:5]
    refs = refs[5:]
    arrays = sum(count for _, count in clips)
    parts, refs = refs[:arrays], refs[arrays:]
    last = len(clips) == 1
    if last:
        before, keep_ref, give_ref, hidden_buf, grad_buf, total_buf, sems = refs
    else:
        total_ref, hidden_buf, grad_buf, sems = refs
    sources = []
    buffers = []
    half = NY // 2
    for i, (r, count) in enumerate(clips):
        across = hidden_top.at[r] if r < half else hidden_bottom.at[r - half]
        for d, source in enumerate((hidden_own.at[r], hidden_up.at[r], across, hidden_down.at[r])):
            sources.append(source)
            buffers.append(hidden_buf.at[i, lax.rem(x_ref[0] + d, NX)])
        size = NX // count
        buffers += [grad_buf.at[i, pl.ds(k * size, size)] for k in range(count)]
        sources += parts[:count]
        parts = parts[count:]
    if last:
        sources.append(before)
        buffers.append(total_buf)
    copies = stage(sources, buffers, sems)
    total = 0.0
    for i, (_, count) in enumerate(clips):
        for copy in copies[: count + NX]:
            copy.wait()
        copies = copies[count + NX :]
        left = hidden_buf[i].reshape(-1, hidden_buf.shape[3])
        right = grad_buf[i].reshape(-1, grad_buf.shape[3])
        total = total + jnp.dot(left.T, right, preferred_element_type=F32)
    if last:
        width = keep_ref.shape[0]
        copies[0].wait()
        total = total + total_buf[...]
        keep_ref[...] = total[:width].astype(BF16)
        give_ref[...] = total[width:].astype(BF16)
    else:
        total_ref[...] = total


def first_gradient(clips, x, hidden, grads, *before):
    _, tokens, width = hidden[0].shape
    cols = grads[0].shape[2]
    if before:
        out_shape = (jax.ShapeDtypeStruct((width // 2, cols), BF16),) * 2
    else:
        out_shape = jax.ShapeDtypeStruct((width, cols), F32)
    return pl.pallas_call(
        functools.partial(first_kernel, clips),
        out_shape=out_shape,
        in_specs=[pl.BlockSpec(memory_space=pltpu.SMEM)]
        + [pl.BlockSpec(memory_space=pl.ANY)] * (len(hidden) + len(grads) + len(before)),
        out_specs=(vmem_spec(), vmem_spec()) if before else vmem_spec(),
        scratch_shapes=[
            pltpu.VMEM((len(clips), NX, tokens, width), BF16),
            pltpu.VMEM((len(clips), NX, tokens, cols), BF16),
            *[pltpu.VMEM(total.shape, F32) for total in before],
            pltpu.SemaphoreType.DMA((NX * len(clips) + len(grads) + len(before),)),
        ],
        compiler_params=params(56),
        cost_estimate=SMALL,
        name="first",
    )(x.reshape(1), *hidden, *grads, *before)


def arrange_kernel(own_ref, other_ref, second_ref, out_ref):
    first = own_ref[...].astype(F32) + other_ref[...].astype(F32)
    second = second_ref[0].astype(F32)
    for x in range(1, NX):
        second = second + second_ref[x].astype(F32)
    for z in range(NZ):
        row = 0
        for total in (first.astype(BF16), second.astype(BF16)):
            rows = total.shape[0] // NZ
            for lane in range(total.shape[1] // LANES):
                out_ref[z // 2, z % 2, row : row + rows, :] = total[
                    z * rows : (z + 1) * rows, lane * LANES : (lane + 1) * LANES
                ]
                row += rows


def arrange(own, other, second):
    rows = (own.size + second[0].size) // (NZ * LANES)
    return pl.pallas_call(
        arrange_kernel,
        out_shape=jax.ShapeDtypeStruct((NZ // 2, 2, rows, LANES), BF16),
        in_specs=[vmem_spec()] * 3,
        out_specs=vmem_spec(),
        compiler_params=params(16),
        cost_estimate=SMALL,
        name="arrange",
    )(own, other, second)


def part_kernel(parity_ref, blocks_ref, keep_ref, give_ref):
    for index, ref in ((parity_ref[0], keep_ref), (1 - parity_ref[0], give_ref)):
        total = blocks_ref[0, index].astype(F32)
        for pair in range(1, NZ // 2):
            total = total + blocks_ref[pair, index].astype(F32)
        ref[...] = total.astype(ref.dtype)


def part(parity, blocks):
    return pl.pallas_call(
        part_kernel,
        out_shape=(
            jax.ShapeDtypeStruct(blocks.shape[2:], F32),
            jax.ShapeDtypeStruct(blocks.shape[2:], BF16),
        ),
        in_specs=[pl.BlockSpec(memory_space=pltpu.SMEM), vmem_spec()],
        out_specs=(vmem_spec(), vmem_spec()),
        compiler_params=params(16),
        cost_estimate=SMALL,
        name="part",
    )(parity.reshape(1), blocks)


def unpack_kernel(place_ref, *refs):
    *parts, first_ref, second_ref = refs
    for index, part in enumerate(parts):
        column = lax.rem(place_ref[0] + index // 2, NX)
        parity = lax.rem(place_ref[1] + index % 2, 2)
        for pair in range(NZ // 2):
            z = 2 * pair + parity
            row = 0
            for ref in (first_ref, second_ref):
                rows = ref.shape[0] // NZ
                cols = ref.shape[1] // NX
                to_row = pl.multiple_of(z * rows, rows)
                for lane in range(cols // LANES):
                    to_lane = pl.multiple_of(column * cols + lane * LANES, LANES)
                    ref[pl.ds(to_row, rows), pl.ds(to_lane, LANES)] = part[
                        pair, row : row + rows, :
                    ]
                    row += rows


def unpack(place, parts, first_shape, second_shape):
    return pl.pallas_call(
        unpack_kernel,
        out_shape=(
            jax.ShapeDtypeStruct(first_shape, BF16),
            jax.ShapeDtypeStruct(second_shape, BF16),
        ),
        in_specs=[pl.BlockSpec(memory_space=pltpu.SMEM)] + [vmem_spec()] * len(parts),
        out_specs=(vmem_spec(), vmem_spec()),
        compiler_params=params(16),
        cost_estimate=SMALL,
        name="unpack",
    )(place, *parts)


def after(values, *others):
    return lax.optimization_barrier((values, others))[0]


def body(
    query_in,
    key_in,
    value_in,
    residual,
    out_proj,
    first_proj,
    first_bias,
    second_proj,
    second_bias,
    teacher,
    teach_index,
    teach_weight,
):
    dp = lax.axis_index("dp")
    seq = lax.axis_index("seq")
    y, core = dp // 2, lax.rem(dp, 2)
    x = seq // NZ
    tokens = query_in.shape[1]
    width = residual.shape[2]
    hid = first_bias.shape[0]
    outf = second_bias.shape[0]

    swap = functools.partial(lax.ppermute, axis_name="dp", perm=core_swap())

    def from_y(value, by):
        return lax.ppermute(value, "dp", dp_shift(-by))

    seconds = [second_proj, from_y(second_proj, 1), from_y(second_proj, 3)]
    middle = second_proj.shape[0] // 2
    seconds += [from_y(seconds[1][:middle], 1), from_y(seconds[2][middle:], 3)]
    peers = [swap(second_proj)]
    out_wide = jnp.concatenate([out_proj, swap(out_proj)], axis=1)
    first_wide = jnp.concatenate([first_proj, swap(first_proj)], axis=0)
    by_core = residual.reshape(NY, 2, tokens, width)
    mine = lax.dynamic_index_in_dim(by_core, core, 1, keepdims=False)
    theirs = lax.dynamic_index_in_dim(by_core, 1 - core, 1, keepdims=False)
    residual_wide = jnp.concatenate([mine, swap(theirs)], axis=2)

    local = teacher[0]
    rows = local.shape[0]
    count = lax.axis_size("seq")
    earlier = lax.ppermute(local, "seq", [(i, i + 1) for i in range(count - 1)])
    later = lax.ppermute(local, "seq", [(i + 1, i) for i in range(count - 1)])
    window = jnp.concatenate([earlier, local, later], axis=0)
    offsets = teach_index - (seq - 1) * rows
    spots = jnp.arange(3 * rows, dtype=jnp.int32)
    blend = jnp.sum(
        jnp.where(offsets[:, :, None] == spots, teach_weight[:, :, None], 0.0), axis=1
    )

    qkv = lax.all_to_all(
        pack(query_in[0], key_in[0], value_in[0]), "seq", 0, 0, tiled=True
    )
    qkv = after(qkv, out_wide, first_wide, residual_wide, seconds, peers[0])
    attended = lax.all_to_all(attend(qkv), "seq", 0, 0, tiled=True)
    peers += [swap(second) for second in seconds[1:]]
    attended = after(attended.reshape(-1, tokens), peers)

    def from_x(value, by):
        return lax.ppermute(value, "seq", x_shift(-by))

    half = attended.shape[0] // 2
    upper = from_y(attended, 1)
    lower = from_y(attended, 3)
    across = [from_y(upper[:half], 1), from_y(lower[half:], 3)]
    (upper, lower), window = lax.optimization_barrier(((upper, lower), window))
    target = jnp.dot(blend, window.astype(F32), precision=lax.Precision.HIGHEST)
    near, *near_terms = hidden_rows(
        ((0, 1), (1, 1), (3, 1)), y, [attended, upper, lower], residual_wide, out_wide, first_wide
    )
    across = after(across, near)
    hidden, far_term = hidden_rows(
        ((2, 2),), y, across, residual_wide, out_wide, first_wide, near
    )
    terms = [
        near_terms[0],
        lax.ppermute(near_terms[1], "dp", dp_shift(1)),
        lax.ppermute(far_term, "dp", dp_shift(2)),
        lax.ppermute(near_terms[2], "dp", dp_shift(3)),
    ]

    hidden_up = from_x(hidden, 1)
    hidden_down = from_x(hidden, 3)
    terms = after(terms, hidden_up, hidden_down)
    hidden_x = [
        hidden,
        hidden_up,
        hidden_down,
        from_x(hidden_up[: NY // 2], 1),
        from_x(hidden_down[NY // 2 :], 3),
    ]

    *sends, pre_grad, cosine = similar(
        jnp.stack([y, core]), terms, first_bias, seconds + peers, second_bias, target
    )
    pre_grad = after(pre_grad, hidden_x)
    sends = [sends[0]] + [from_y(sends[r], r) for r in range(1, NY)]

    pre_x = lax.all_to_all(pre_grad, "seq", 0, 0, tiled=True, axis_index_groups=X_GROUPS)
    upper = from_y(pre_x, 1)
    lower = from_y(pre_x, 3)
    across = [from_y(upper[: NX // 2], 1), from_y(lower[NX // 2 :], 3)]

    units = second_proj.shape[0]
    keep, give = second_gradient(core, after(sends, pre_x), units, outf)
    second_own = (keep.astype(F32) + swap(give).astype(F32)).astype(BF16)
    second_parts = lax.all_to_all(
        second_own, "seq", 0, 0, tiled=True, axis_index_groups=X_GROUPS
    )
    total = first_gradient(((1, 1), (3, 1), (0, 1)), x, hidden_x, [upper, lower, pre_x])
    across = after(across, total)
    first_own, first_give = first_gradient(((2, 2),), x, hidden_x, across, total)

    z = lax.rem(seq, NZ)
    blocks = arrange(first_own, swap(first_give), second_parts)
    blocks = lax.all_to_all(blocks, "seq", 0, 0, tiled=True, axis_index_groups=PARITY_GROUPS)
    keep, give = part(lax.rem(z, 2), blocks)
    summed = (keep + lax.ppermute(give, "seq", z_swap()).astype(F32)).astype(BF16)

    same = lax.all_gather(summed, "seq", axis=0, axis_index_groups=PARITY_GROUPS)
    other = lax.ppermute(same, "seq", z_swap())
    same_x = {0: same, 1: from_x(same, 1), 3: from_x(same, 3)}
    other_x = {0: other, 1: from_x(other, 1), 3: from_x(other, 3)}
    same_x[2] = from_x(same_x[1], 1)
    other_x[2] = from_x(other_x[3], 3)
    grad_first, grad_second = unpack(
        jnp.stack([x, z]),
        [part for d in range(NX) for part in (same_x[d], other_x[d])],
        (width, hid),
        (units, outf),
    )
    return (cosine.reshape(1, -1), grad_first, grad_second)


def solution(mesh):
    placed = (
        P("dp", "seq", None),
        P("dp", "seq", None),
        P("dp", "seq", None),
        P(None, "seq", "dp"),
        P(None, "dp"),
        P("dp", None),
        P(),
        P("dp", None),
        P(),
        P("dp", "seq", None),
        P("seq", None),
        P("seq", None),
    )
    return jax.shard_map(
        body,
        mesh=mesh,
        in_specs=placed,
        out_specs=(P("dp", "seq"), P("dp", None), P("dp", None)),
        check_vma=False,
    )
```

```python
import functools
import math

import jax
import jax.numpy as jnp
from jax import lax
from jax.experimental import pallas as pl
from jax.experimental.pallas import tpu as pltpu
from jax.sharding import PartitionSpec as P

HEAD_DIM = 64
LANES = 128
EPSILON = 1e-06
SCORE_SCALE = HEAD_DIM ** (-0.5) * math.log2(math.e)
SMALLEST_SUM = 2.0 ** -90
BF16 = jnp.bfloat16
F32 = jnp.float32
NX, NZ, NY = 4, 8, 4
LARGE = pl.CostEstimate(flops=2**35, bytes_accessed=2**23, transcendentals=0)
SMALL = pl.CostEstimate(flops=0, bytes_accessed=0, transcendentals=0)


def dp_shift(by):
    return [(i, (i + 2 * by) % (2 * NY)) for i in range(2 * NY)]


def core_swap():
    return [(i, i ^ 1) for i in range(2 * NY)]


def x_shift(by):
    return [(x * NZ + z, ((x + by) % NX) * NZ + z) for x in range(NX) for z in range(NZ)]


def z_swap():
    return [(i, i ^ 1) for i in range(NX * NZ)]


X_GROUPS = [[x * NZ + z for x in range(NX)] for z in range(NZ)]


def pair_shift(by):
    return [
        (x * NZ + z, x * NZ + (z + 2 * by) % NZ) for x in range(NX) for z in range(NZ)
    ]


def vmem_spec():
    return pl.BlockSpec(memory_space=pltpu.VMEM)


def params(mib):
    return pltpu.CompilerParams(vmem_limit_bytes=mib * 1024 * 1024)


def pack_kernel(query_hbm, key_hbm, value_hbm, out_hbm, in_buf, out_buf, in_sems, out_sems):
    steps = in_sems.shape[0]
    cols = in_buf.shape[2] // steps
    heads = out_buf.shape[0] // steps
    loads = [
        [
            pltpu.make_async_copy(
                source.at[:, pl.ds(step * cols, cols)],
                in_buf.at[which, :, pl.ds(step * cols, cols)],
                in_sems.at[step, which],
            )
            for which, source in enumerate((query_hbm, key_hbm, value_hbm))
        ]
        for step in range(steps)
    ]
    stores = [
        pltpu.make_async_copy(
            out_buf.at[pl.ds(step * heads, heads)],
            out_hbm.at[pl.ds(step * heads, heads)],
            out_sems.at[step],
        )
        for step in range(steps)
    ]
    for step in range(steps):
        for load in loads[step]:
            load.start()
    for step in range(steps):
        for which, load in enumerate(loads[step]):
            load.wait()
            row = which * HEAD_DIM
            for pair in range(step * heads // 2, (step + 1) * heads // 2):
                turned = in_buf[which, :, pair * LANES : (pair + 1) * LANES].T
                out_buf[2 * pair, row : row + HEAD_DIM, :] = turned[:HEAD_DIM]
                out_buf[2 * pair + 1, row : row + HEAD_DIM, :] = turned[HEAD_DIM:]
        stores[step].start()
    for store in stores:
        store.wait()


def pack(query, key, value):
    tokens, width = query.shape
    heads = width // HEAD_DIM
    steps = 4
    hbm = pl.BlockSpec(memory_space=pltpu.HBM)
    return pl.pallas_call(
        pack_kernel,
        out_shape=jax.ShapeDtypeStruct((heads, 3 * HEAD_DIM, tokens), BF16),
        in_specs=[hbm] * 3,
        out_specs=hbm,
        scratch_shapes=[
            pltpu.VMEM((3, tokens, width), BF16),
            pltpu.VMEM((heads, 3 * HEAD_DIM, tokens), BF16),
            pltpu.SemaphoreType.DMA((steps, 3)),
            pltpu.SemaphoreType.DMA((steps,)),
        ],
        compiler_params=params(56),
        cost_estimate=SMALL,
        name="pack",
    )(query, key, value)


Q_ROWS = 512
K_ROWS = 1024
DEPTH = 2 * HEAD_DIM + 16
V_ROWS = HEAD_DIM + 16


def attend_kernel(qkv_ref, out_ref, key_buf, value_buf):
    slabs = qkv_ref.shape[0]
    length = slabs * LANES
    per_block = Q_ROWS // LANES
    largest = jnp.zeros((1, LANES), F32)
    for slab in range(slabs):
        rows = slice(slab * LANES, (slab + 1) * LANES)
        keys = qkv_ref[slab, HEAD_DIM : 2 * HEAD_DIM, :]
        turned = keys.T
        key_buf[rows, 0:HEAD_DIM] = turned
        key_buf[rows, HEAD_DIM : 2 * HEAD_DIM] = turned
        wide = keys.astype(F32)
        largest = jnp.maximum(largest, jnp.sum(wide * wide, axis=0, keepdims=True))
        value_buf[0:HEAD_DIM, rows] = qkv_ref[slab, 2 * HEAD_DIM : 3 * HEAD_DIM, :]
    key_buf[:, 2 * HEAD_DIM : DEPTH] = jnp.ones((length, DEPTH - 2 * HEAD_DIM), BF16)
    value_buf[HEAD_DIM:V_ROWS, :] = jnp.ones((V_ROWS - HEAD_DIM, length), BF16)
    key_bound = jnp.max(largest, axis=1, keepdims=True)

    def load_queries(block):
        return jnp.concatenate(
            [qkv_ref[block * per_block + j, 0:HEAD_DIM, :] for j in range(per_block)], axis=1
        )

    def store(block, total):
        result = (total[0:HEAD_DIM] / total[HEAD_DIM : HEAD_DIM + 1]).astype(BF16)
        for j in range(per_block):
            out_ref[block * per_block + j] = result[:, j * LANES : (j + 1) * LANES]

    first_row = lax.broadcasted_iota(jnp.int32, (DEPTH - 2 * HEAD_DIM, Q_ROWS), 0) == 0

    def step(block, least):
        queries = load_queries(block).astype(F32)
        bound = SCORE_SCALE * jnp.sqrt(
            jnp.sum(queries * queries, axis=0, keepdims=True) * key_bound
        )
        scaled = queries * SCORE_SCALE
        high = scaled.astype(BF16)
        low = (scaled - high.astype(F32)).astype(BF16)
        shift = jnp.where(first_row, -bound, 0.0).astype(BF16)
        stacked = jnp.concatenate([high, low, shift], axis=0)
        total = jnp.zeros((V_ROWS, Q_ROWS), F32)
        for part in range(length // K_ROWS):
            span = slice(part * K_ROWS, (part + 1) * K_ROWS)
            scores = jnp.dot(key_buf[span, :], stacked, preferred_element_type=F32)
            weights = jnp.exp2(scores).astype(BF16)
            total = total + jnp.dot(value_buf[:, span], weights, preferred_element_type=F32)
        store(block, total)
        return jnp.minimum(least, total[HEAD_DIM : HEAD_DIM + 1])

    least = lax.fori_loop(0, length // Q_ROWS, step, jnp.full((1, Q_ROWS), 1.0, F32))

    @pl.when(jnp.min(least) < SMALLEST_SUM)
    def _():
        def careful(block, _):
            queries = load_queries(block)

            def inner(part, state):
                top, total = state
                begin = pl.multiple_of(part * K_ROWS, K_ROWS)
                keys = key_buf[pl.ds(begin, K_ROWS), 0:HEAD_DIM]
                scores = jnp.dot(keys, queries, preferred_element_type=F32)
                higher = jnp.maximum(top, jnp.max(scores, axis=0, keepdims=True))
                weights = jnp.exp2((scores - higher) * SCORE_SCALE).astype(BF16)
                fade = jnp.exp2((top - higher) * SCORE_SCALE)
                added = jnp.dot(
                    value_buf[:, pl.ds(begin, K_ROWS)], weights, preferred_element_type=F32
                )
                return higher, total * fade + added

            start = (jnp.full((1, Q_ROWS), -1e30, F32), jnp.zeros((V_ROWS, Q_ROWS), F32))
            _, total = lax.fori_loop(0, length // K_ROWS, inner, start)
            store(block, total)
            return 0

        lax.fori_loop(0, length // Q_ROWS, careful, 0)


def attend(qkv):
    slabs = qkv.shape[0]
    length = slabs * LANES
    return pl.pallas_call(
        attend_kernel,
        out_shape=jax.ShapeDtypeStruct((slabs, HEAD_DIM, LANES), BF16),
        in_specs=[vmem_spec()],
        out_specs=vmem_spec(),
        scratch_shapes=[pltpu.VMEM((length, DEPTH), BF16), pltpu.VMEM((V_ROWS, length), BF16)],
        compiler_params=params(20),
        cost_estimate=SMALL,
        name="attend",
    )(qkv)


def stage(sources, buffers, sems):
    copies = [
        pltpu.make_async_copy(source, buffer, sems.at[i])
        for i, (source, buffer) in enumerate(zip(sources, buffers))
    ]
    for copy in copies:
        copy.start()
    return copies


def hidden_kernel(pieces, y_ref, *refs):
    arrays = sum(count for _, count in pieces)
    clips = len(pieces)
    parts, refs = refs[:arrays], refs[arrays:]
    residual, out_hbm, first_hbm = refs[:3]
    near = () if clips > 1 else refs[3:4]
    refs = refs[3 + len(near) :]
    hidden_ref, *terms = refs[: 1 + clips]
    rows_buf, residual_buf, out_buf, first_buf, hidden_buf, sems = refs[1 + clips :]
    inner = out_buf.shape[0]
    chunks = 4
    depth = inner // chunks
    span = first_buf.shape[0] // 2
    sources = list(parts) + [residual]
    buffers = []
    for clip, (_, count) in enumerate(pieces):
        size = inner // count
        buffers += [rows_buf.at[clip, pl.ds(k * size, size)] for k in range(count)]
    buffers.append(residual_buf)
    for k in range(chunks):
        sources.append(out_hbm.at[pl.ds(k * depth, depth)])
        buffers.append(out_buf.at[pl.ds(k * depth, depth)])
    for k in range(2):
        sources.append(first_hbm.at[pl.ds(k * span, span)])
        buffers.append(first_buf.at[pl.ds(k * span, span)])
    if near:
        sources += [near[0].at[pl.ds(0, 2)], near[0].at[2]]
        buffers += [hidden_buf.at[pl.ds(0, 2)], hidden_buf.at[3]]
    copies = stage(sources, buffers, sems)
    for copy in copies[: arrays + 1]:
        copy.wait()
    tokens = rows_buf.shape[2]
    mixed = jnp.concatenate(
        [residual_buf[lax.rem(y_ref[0] + r, NY)].astype(F32) for r, _ in pieces], axis=0
    )
    for k in range(chunks):
        part = slice(k * depth, (k + 1) * depth)
        rows = jnp.concatenate([rows_buf[clip, part, :].T for clip in range(clips)], axis=0)
        copies[arrays + 1 + k].wait()
        mixed = mixed + jnp.dot(rows, out_buf[part, :], preferred_element_type=F32)
    hidden = mixed.astype(BF16)
    for clip in range(clips):
        hidden_buf[2 if near else clip] = hidden[clip * tokens : (clip + 1) * tokens]
    for copy in copies[arrays + 1 + chunks :]:
        copy.wait()
    last = pltpu.make_async_copy(hidden_buf, hidden_ref, sems.at[len(sources)])
    last.start()
    for clip, ref in enumerate(terms):
        rows = hidden[clip * tokens : (clip + 1) * tokens]
        ref[...] = jnp.dot(rows, first_buf[...], preferred_element_type=F32).astype(BF16)
    last.wait()


def hidden_rows(pieces, y, parts, residual, out_wide, first_wide, *near):
    inner = out_wide.shape[0]
    tokens = parts[0].shape[1]
    width, hid = first_wide.shape
    clips = len(pieces)
    return pl.pallas_call(
        functools.partial(hidden_kernel, pieces),
        out_shape=(
            jax.ShapeDtypeStruct((NY if near else clips, tokens, width), BF16),
            *[jax.ShapeDtypeStruct((tokens, hid), BF16)] * clips,
        ),
        in_specs=[pl.BlockSpec(memory_space=pltpu.SMEM)]
        + [pl.BlockSpec(memory_space=pl.ANY)] * (3 + len(parts) + len(near)),
        out_specs=(pl.BlockSpec(memory_space=pl.ANY), *[vmem_spec()] * clips),
        scratch_shapes=[
            pltpu.VMEM((clips, inner, tokens), BF16),
            pltpu.VMEM((NY, tokens, width), BF16),
            pltpu.VMEM((inner, width), BF16),
            pltpu.VMEM((width, hid), BF16),
            pltpu.VMEM((NY if near else clips, tokens, width), BF16),
            pltpu.SemaphoreType.DMA((len(parts) + 8 + 2 * len(near),)),
        ],
        compiler_params=params(56),
        cost_estimate=SMALL,
        name="hidden",
    )(y.reshape(1), *parts, residual, out_wide, first_wide, *near)


def similar_kernel(
    place_ref, own_hbm, one_hbm, two_hbm, three_hbm, target_hbm, own_0, own_1, own_3, own_2, own_2b,
    peer_0, peer_1, peer_3, peer_2, peer_2b, first_bias_ref, second_bias_ref, send_0, send_1, send_2, send_3, pre_grad_ref, cosine_ref,
    terms_ref, target_ref, second_ref, active_ref, slope_ref, sems,
):
    hid, outf = second_ref.shape
    depth = own_0.shape[0]
    sources = [own_hbm, one_hbm, two_hbm, three_hbm]
    buffers = [terms_ref.at[r] for r in range(NY)]
    spans = []
    for parity, second in (
        (place_ref[1], (own_0, own_1, own_3, own_2, own_2b)),
        (1 - place_ref[1], (peer_0, peer_1, peer_3, peer_2, peer_2b)),
    ):
        for piece, r in zip(second, (0, 1, 3, 2, 2)):
            rows = piece.shape[0]
            owner = 2 * lax.rem(place_ref[0] + r, NY) + parity
            begin = owner * depth + (rows if piece is second[-1] else 0)
            spans.append(pl.ds(pl.multiple_of(begin, rows), rows))
            sources.append(piece)
            buffers.append(second_ref.at[spans[-1]])
    copies = stage(sources + [target_hbm], buffers + [target_ref], sems)
    for copy in copies[:NY]:
        copy.wait()
    preact = first_bias_ref[...] + sum(terms_ref[r].astype(F32) for r in range(NY))
    gate = 1.0 / (1.0 + jnp.exp(-preact))
    active_ref[...] = (preact * gate).astype(BF16)
    slope_ref[...] = gate * (1.0 + preact * (1.0 - gate))
    projected = jnp.broadcast_to(second_bias_ref[...], target_ref.shape)
    for k, span in enumerate(spans):
        copies[NY + k].wait()
        projected = projected + jnp.dot(
            active_ref[:, span], second_ref[span, :], preferred_element_type=F32
        )
    copies[-1].wait()
    target = target_ref[...]
    inv_model = lax.rsqrt(jnp.sum(projected * projected, axis=1, keepdims=True) + EPSILON)
    inv_target = lax.rsqrt(jnp.sum(target * target, axis=1, keepdims=True) + EPSILON)
    cosine = jnp.sum(projected * target, axis=1, keepdims=True) * inv_model * inv_target
    cosine_ref[...] = cosine
    row_grad = (
        -math.sqrt(outf) * inv_model * (target * inv_target - cosine * inv_model * projected)
    ).astype(BF16)
    units = hid // NY
    for r, send in enumerate((send_0, send_1, send_2, send_3)):
        chip = lax.rem(place_ref[0] + (NY - r), NY)
        send[:, :units] = active_ref[:, pl.ds(pl.multiple_of(chip * units, units), units)]
        send[:, units:] = row_grad
    cols = hid // NX
    for quarter in range(NX):
        span = slice(quarter * cols, (quarter + 1) * cols)
        back = lax.dot_general(
            row_grad, second_ref[span, :], (((1,), (1,)), ((), ())), preferred_element_type=F32
        )
        pre_grad_ref[quarter] = (back * slope_ref[:, span]).astype(BF16)


def similar(place, terms, first_bias, seconds, second_bias, target):
    tokens, hid = terms[0].shape
    outf = seconds[0].shape[1]
    send = jax.ShapeDtypeStruct((tokens, hid // NY + outf), BF16)
    specs = [pl.BlockSpec(memory_space=pl.ANY)] * (NY + 1 + len(seconds)) + [vmem_spec()] * 2
    return pl.pallas_call(
        similar_kernel,
        out_shape=(
            (send,) * NY
            + (
                jax.ShapeDtypeStruct((NX, tokens, hid // NX), BF16),
                jax.ShapeDtypeStruct((tokens, 1), F32),
            )
        ),
        in_specs=[pl.BlockSpec(memory_space=pltpu.SMEM)] + specs,
        out_specs=(vmem_spec(),) * (NY + 2),
        scratch_shapes=[
            pltpu.VMEM((NY, tokens, hid), BF16),
            pltpu.VMEM((tokens, outf), F32),
            pltpu.VMEM((hid, outf), BF16),
            pltpu.VMEM((tokens, hid), BF16),
            pltpu.VMEM((tokens, hid), F32),
            pltpu.SemaphoreType.DMA((NY + 1 + len(seconds),)),
        ],
        compiler_params=params(56),
        cost_estimate=SMALL,
        name="similar",
    )(
        place, *terms, target, *seconds, first_bias.reshape(1, -1),
        second_bias.reshape(1, -1),
    )


def second_kernel(core_ref, one, two, three, four, keep_ref, give_ref):
    units = 2 * keep_ref.shape[1]
    cols = keep_ref.shape[2]
    parts = (one, two, three, four)
    active = jnp.concatenate([part[:, :units] for part in parts], axis=0).T
    grads = [
        jnp.concatenate(
            [part[:, units + x * cols : units + (x + 1) * cols] for part in parts], axis=0
        )
        for x in range(NX)
    ]
    half = units // 2
    for x in range(NX):
        total = jnp.dot(active, grads[x], preferred_element_type=F32).astype(BF16)
        top, bottom = total[:half], total[half:]
        first = core_ref[0] == 0
        keep_ref[x] = jnp.where(first, top, bottom)
        give_ref[x] = jnp.where(first, bottom, top)


def second_gradient(core, parts, units, outf):
    shape = jax.ShapeDtypeStruct((NX, units, outf // NX), BF16)
    return pl.pallas_call(
        second_kernel,
        out_shape=(shape, shape),
        in_specs=[pl.BlockSpec(memory_space=pltpu.SMEM)] + [vmem_spec()] * NY,
        out_specs=(vmem_spec(), vmem_spec()),
        compiler_params=params(24),
        cost_estimate=LARGE,
        name="second",
    )(core.reshape(1), *parts)


def first_kernel(clips, x_ref, *refs):
    hidden_own, hidden_up, hidden_down, hidden_top, hidden_bottom = refs[:5]
    refs = refs[5:]
    arrays = sum(count for _, count in clips)
    parts, refs = refs[:arrays], refs[arrays:]
    last = len(clips) == 1
    if last:
        before, keep_ref, give_ref, hidden_buf, grad_buf, total_buf, sems = refs
    else:
        total_ref, hidden_buf, grad_buf, sems = refs
    sources = []
    buffers = []
    half = NY // 2
    for i, (r, count) in enumerate(clips):
        across = hidden_top.at[r] if r < half else hidden_bottom.at[r - half]
        for d, source in enumerate((hidden_own.at[r], hidden_up.at[r], across, hidden_down.at[r])):
            sources.append(source)
            buffers.append(hidden_buf.at[i, lax.rem(x_ref[0] + d, NX)])
        size = NX // count
        buffers += [grad_buf.at[i, pl.ds(k * size, size)] for k in range(count)]
        sources += parts[:count]
        parts = parts[count:]
    if last:
        sources.append(before)
        buffers.append(total_buf)
    copies = stage(sources, buffers, sems)
    total = 0.0
    for i, (_, count) in enumerate(clips):
        for copy in copies[: count + NX]:
            copy.wait()
        copies = copies[count + NX :]
        left = hidden_buf[i].reshape(-1, hidden_buf.shape[3])
        right = grad_buf[i].reshape(-1, grad_buf.shape[3])
        total = total + jnp.dot(left.T, right, preferred_element_type=F32)
    if last:
        width = keep_ref.shape[0]
        copies[0].wait()
        total = total + total_buf[...]
        keep_ref[...] = total[:width].astype(BF16)
        give_ref[...] = total[width:].astype(BF16)
    else:
        total_ref[...] = total


def first_gradient(clips, x, hidden, grads, *before):
    _, tokens, width = hidden[0].shape
    cols = grads[0].shape[2]
    if before:
        out_shape = (jax.ShapeDtypeStruct((width // 2, cols), BF16),) * 2
    else:
        out_shape = jax.ShapeDtypeStruct((width, cols), F32)
    return pl.pallas_call(
        functools.partial(first_kernel, clips),
        out_shape=out_shape,
        in_specs=[pl.BlockSpec(memory_space=pltpu.SMEM)]
        + [pl.BlockSpec(memory_space=pl.ANY)] * (len(hidden) + len(grads) + len(before)),
        out_specs=(vmem_spec(), vmem_spec()) if before else vmem_spec(),
        scratch_shapes=[
            pltpu.VMEM((len(clips), NX, tokens, width), BF16),
            pltpu.VMEM((len(clips), NX, tokens, cols), BF16),
            *[pltpu.VMEM(total.shape, F32) for total in before],
            pltpu.SemaphoreType.DMA((NX * len(clips) + len(grads) + len(before),)),
        ],
        compiler_params=params(56),
        cost_estimate=SMALL,
        name="first",
    )(x.reshape(1), *hidden, *grads, *before)


def arrange_kernel(pair_ref, own_ref, other_ref, second_ref, *refs):
    *outs, first_sum, second_sum = refs
    first_sum[...] = (own_ref[...].astype(F32) + other_ref[...].astype(F32)).astype(BF16)
    second = second_ref[0].astype(F32)
    for x in range(1, NX):
        second = second + second_ref[x].astype(F32)
    second_sum[...] = second.astype(BF16)
    for step, out_ref in enumerate(outs):
        pair = lax.rem(pair_ref[0] + step, NZ // 2)
        for parity in range(2):
            row = 0
            for total in (first_sum, second_sum):
                rows = total.shape[0] // NZ
                begin = pl.multiple_of((2 * pair + parity) * rows, rows)
                for lane in range(total.shape[1] // LANES):
                    out_ref[parity, row : row + rows, :] = total[
                        pl.ds(begin, rows), lane * LANES : (lane + 1) * LANES
                    ]
                    row += rows


def arrange(pair, own, other, second):
    rows = (own.size + second[0].size) // (NZ * LANES)
    return pl.pallas_call(
        arrange_kernel,
        out_shape=(jax.ShapeDtypeStruct((2, rows, LANES), BF16),) * (NZ // 2),
        in_specs=[pl.BlockSpec(memory_space=pltpu.SMEM)] + [vmem_spec()] * 3,
        out_specs=(vmem_spec(),) * (NZ // 2),
        scratch_shapes=[pltpu.VMEM(own.shape, BF16), pltpu.VMEM(second.shape[1:], BF16)],
        compiler_params=params(16),
        cost_estimate=SMALL,
        name="arrange",
    )(pair.reshape(1), own, other, second)


def part_kernel(parity_ref, *refs):
    *blocks, keep_ref, give_ref = refs
    for index, ref in ((parity_ref[0], keep_ref), (1 - parity_ref[0], give_ref)):
        ref[...] = sum(block[index].astype(F32) for block in blocks).astype(ref.dtype)


def part(parity, blocks):
    shape = blocks[0].shape[1:]
    return pl.pallas_call(
        part_kernel,
        out_shape=(jax.ShapeDtypeStruct(shape, F32), jax.ShapeDtypeStruct(shape, BF16)),
        in_specs=[pl.BlockSpec(memory_space=pltpu.SMEM)] + [vmem_spec()] * len(blocks),
        out_specs=(vmem_spec(), vmem_spec()),
        compiler_params=params(16),
        cost_estimate=SMALL,
        name="part",
    )(parity.reshape(1), *blocks)


def unpack_kernel(place_ref, *refs):
    *parts, first_ref, second_ref = refs
    for index, part in enumerate(parts):
        column = lax.rem(place_ref[0] + index // 2, NX)
        parity = lax.rem(place_ref[1] + index % 2, 2)
        for pair in range(NZ // 2):
            z = 2 * lax.rem(place_ref[1] // 2 + pair, NZ // 2) + parity
            row = 0
            for ref in (first_ref, second_ref):
                rows = ref.shape[0] // NZ
                cols = ref.shape[1] // NX
                to_row = pl.multiple_of(z * rows, rows)
                for lane in range(cols // LANES):
                    to_lane = pl.multiple_of(column * cols + lane * LANES, LANES)
                    ref[pl.ds(to_row, rows), pl.ds(to_lane, LANES)] = part[
                        pair, row : row + rows, :
                    ]
                    row += rows


def unpack(place, parts, first_shape, second_shape):
    return pl.pallas_call(
        unpack_kernel,
        out_shape=(
            jax.ShapeDtypeStruct(first_shape, BF16),
            jax.ShapeDtypeStruct(second_shape, BF16),
        ),
        in_specs=[pl.BlockSpec(memory_space=pltpu.SMEM)] + [vmem_spec()] * len(parts),
        out_specs=(vmem_spec(), vmem_spec()),
        compiler_params=params(16),
        cost_estimate=SMALL,
        name="unpack",
    )(place, *parts)


def after(values, *others):
    return lax.optimization_barrier((values, others))[0]


def body(
    query_in,
    key_in,
    value_in,
    residual,
    out_proj,
    first_proj,
    first_bias,
    second_proj,
    second_bias,
    teacher,
    teach_index,
    teach_weight,
):
    dp = lax.axis_index("dp")
    seq = lax.axis_index("seq")
    y, core = dp // 2, lax.rem(dp, 2)
    x = seq // NZ
    tokens = query_in.shape[1]
    width = residual.shape[2]
    hid = first_bias.shape[0]
    outf = second_bias.shape[0]

    swap = functools.partial(lax.ppermute, axis_name="dp", perm=core_swap())

    def from_y(value, by):
        return lax.ppermute(value, "dp", dp_shift(-by))

    seconds = [second_proj, from_y(second_proj, 1), from_y(second_proj, 3)]
    middle = second_proj.shape[0] // 2
    seconds += [from_y(seconds[1][:middle], 1), from_y(seconds[2][middle:], 3)]
    peers = [swap(second_proj)]
    out_wide = jnp.concatenate([out_proj, swap(out_proj)], axis=1)
    first_wide = jnp.concatenate([first_proj, swap(first_proj)], axis=0)
    by_core = residual.reshape(NY, 2, tokens, width)
    mine = lax.dynamic_index_in_dim(by_core, core, 1, keepdims=False)
    theirs = lax.dynamic_index_in_dim(by_core, 1 - core, 1, keepdims=False)
    residual_wide = jnp.concatenate([mine, swap(theirs)], axis=2)

    local = teacher[0]
    rows = local.shape[0]
    count = lax.axis_size("seq")
    earlier = lax.ppermute(local, "seq", [(i, i + 1) for i in range(count - 1)])
    later = lax.ppermute(local, "seq", [(i + 1, i) for i in range(count - 1)])
    window = jnp.concatenate([earlier, local, later], axis=0)
    offsets = teach_index - (seq - 1) * rows
    spots = jnp.arange(3 * rows, dtype=jnp.int32)
    blend = jnp.sum(
        jnp.where(offsets[:, :, None] == spots, teach_weight[:, :, None], 0.0), axis=1
    )

    qkv = lax.all_to_all(
        pack(query_in[0], key_in[0], value_in[0]), "seq", 0, 0, tiled=True
    )
    qkv = after(qkv, out_wide, first_wide, residual_wide, seconds, peers[0])
    attended = lax.all_to_all(attend(qkv), "seq", 0, 0, tiled=True)
    peers += [swap(second) for second in seconds[1:]]
    attended = after(attended.reshape(-1, tokens), peers)

    def from_x(value, by):
        return lax.ppermute(value, "seq", x_shift(-by))

    half = attended.shape[0] // 2
    upper = from_y(attended, 1)
    lower = from_y(attended, 3)
    across = [from_y(upper[:half], 1), from_y(lower[half:], 3)]
    (upper, lower), window = lax.optimization_barrier(((upper, lower), window))
    target = jnp.dot(blend, window.astype(F32), precision=lax.Precision.HIGHEST)
    near, *near_terms = hidden_rows(
        ((0, 1), (1, 1), (3, 1)), y, [attended, upper, lower], residual_wide, out_wide, first_wide
    )
    across = after(across, near)
    hidden, far_term = hidden_rows(
        ((2, 2),), y, across, residual_wide, out_wide, first_wide, near
    )
    terms = [
        near_terms[0],
        lax.ppermute(near_terms[1], "dp", dp_shift(1)),
        lax.ppermute(far_term, "dp", dp_shift(2)),
        lax.ppermute(near_terms[2], "dp", dp_shift(3)),
    ]

    hidden_up = from_x(hidden, 1)
    hidden_down = from_x(hidden, 3)
    terms = after(terms, hidden_up, hidden_down)
    hidden_x = [
        hidden,
        hidden_up,
        hidden_down,
        from_x(hidden_up[: NY // 2], 1),
        from_x(hidden_down[NY // 2 :], 3),
    ]

    *sends, pre_grad, cosine = similar(
        jnp.stack([y, core]), terms, first_bias, seconds + peers, second_bias, target
    )
    pre_grad = after(pre_grad, hidden_x)
    sends = [sends[0]] + [from_y(sends[r], r) for r in range(1, NY)]

    pre_x = lax.all_to_all(pre_grad, "seq", 0, 0, tiled=True, axis_index_groups=X_GROUPS)
    upper = from_y(pre_x, 1)
    lower = from_y(pre_x, 3)
    across = [from_y(upper[: NX // 2], 1), from_y(lower[NX // 2 :], 3)]

    units = second_proj.shape[0]
    keep, give = second_gradient(core, after(sends, pre_x), units, outf)
    second_own = (keep.astype(F32) + swap(give).astype(F32)).astype(BF16)
    second_parts = lax.all_to_all(
        second_own, "seq", 0, 0, tiled=True, axis_index_groups=X_GROUPS
    )
    total = first_gradient(((1, 1), (3, 1), (0, 1)), x, hidden_x, [upper, lower, pre_x])
    across = after(across, total)
    first_own, first_give = first_gradient(((2, 2),), x, hidden_x, across, total)

    z = lax.rem(seq, NZ)
    blocks = arrange(z // 2, first_own, swap(first_give), second_parts)

    def from_pair(value, by):
        return lax.ppermute(value, "seq", pair_shift(-by))

    blocks = [blocks[0]] + [from_pair(blocks[k], -k) for k in (1, 3, 2)]
    keep, give = part(lax.rem(z, 2), blocks)
    summed = (keep + lax.ppermute(give, "seq", z_swap()).astype(F32)).astype(BF16)

    same = jnp.stack([summed] + [from_pair(summed, k) for k in range(1, NZ // 2)])
    other = lax.ppermute(same, "seq", z_swap())
    same_x = {0: same, 1: from_x(same, 1), 3: from_x(same, 3)}
    other_x = {0: other, 1: from_x(other, 1), 3: from_x(other, 3)}
    same_x[2] = from_x(same_x[1], 1)
    other_x[2] = from_x(other_x[3], 3)
    grad_first, grad_second = unpack(
        jnp.stack([x, z]),
        [part for d in range(NX) for part in (same_x[d], other_x[d])],
        (width, hid),
        (units, outf),
    )
    return (cosine.reshape(1, -1), grad_first, grad_second)


def solution(mesh):
    placed = (
        P("dp", "seq", None),
        P("dp", "seq", None),
        P("dp", "seq", None),
        P(None, "seq", "dp"),
        P(None, "dp"),
        P("dp", None),
        P(),
        P("dp", None),
        P(),
        P("dp", "seq", None),
        P("seq", None),
        P("seq", None),
    )
    return jax.shard_map(
        body,
        mesh=mesh,
        in_specs=placed,
        out_specs=(P("dp", "seq"), P("dp", None), P("dp", None)),
        check_vma=False,
    )
```

```python
import functools
import math

import jax
import jax.numpy as jnp
from jax import lax
from jax.experimental import pallas as pl
from jax.experimental.pallas import tpu as pltpu
from jax.sharding import PartitionSpec as P

HEAD_DIM = 64
LANES = 128
EPSILON = 1e-06
SCORE_SCALE = HEAD_DIM ** (-0.5) * math.log2(math.e)
SMALLEST_SUM = 2.0 ** -90
BF16 = jnp.bfloat16
F32 = jnp.float32
NX, NZ, NY = 4, 8, 4
LARGE = pl.CostEstimate(flops=2**35, bytes_accessed=2**23, transcendentals=0)
SMALL = pl.CostEstimate(flops=0, bytes_accessed=0, transcendentals=0)


def dp_shift(by):
    return [(i, (i + 2 * by) % (2 * NY)) for i in range(2 * NY)]


def core_swap():
    return [(i, i ^ 1) for i in range(2 * NY)]


def x_shift(by):
    return [(x * NZ + z, ((x + by) % NX) * NZ + z) for x in range(NX) for z in range(NZ)]


def z_swap():
    return [(i, i ^ 1) for i in range(NX * NZ)]


X_GROUPS = [[x * NZ + z for x in range(NX)] for z in range(NZ)]


def pair_shift(by):
    return [
        (x * NZ + z, x * NZ + (z + 2 * by) % NZ) for x in range(NX) for z in range(NZ)
    ]


def vmem_spec():
    return pl.BlockSpec(memory_space=pltpu.VMEM)


def params(mib):
    return pltpu.CompilerParams(vmem_limit_bytes=mib * 1024 * 1024)


def pack_kernel(query_hbm, key_hbm, value_hbm, out_hbm, in_buf, out_buf, in_sems, out_sems):
    steps = in_sems.shape[0]
    cols = in_buf.shape[2] // steps
    heads = out_buf.shape[0] // steps
    loads = [
        [
            pltpu.make_async_copy(
                source.at[:, pl.ds(step * cols, cols)],
                in_buf.at[which, :, pl.ds(step * cols, cols)],
                in_sems.at[step, which],
            )
            for which, source in enumerate((query_hbm, key_hbm, value_hbm))
        ]
        for step in range(steps)
    ]
    stores = [
        pltpu.make_async_copy(
            out_buf.at[pl.ds(step * heads, heads)],
            out_hbm.at[pl.ds(step * heads, heads)],
            out_sems.at[step],
        )
        for step in range(steps)
    ]
    for step in range(steps):
        for load in loads[step]:
            load.start()
    for step in range(steps):
        for which, load in enumerate(loads[step]):
            load.wait()
            row = which * HEAD_DIM
            for pair in range(step * heads // 2, (step + 1) * heads // 2):
                turned = in_buf[which, :, pair * LANES : (pair + 1) * LANES].T
                out_buf[2 * pair, row : row + HEAD_DIM, :] = turned[:HEAD_DIM]
                out_buf[2 * pair + 1, row : row + HEAD_DIM, :] = turned[HEAD_DIM:]
        stores[step].start()
    for store in stores:
        store.wait()


def pack(query, key, value):
    tokens, width = query.shape
    heads = width // HEAD_DIM
    steps = 4
    hbm = pl.BlockSpec(memory_space=pltpu.HBM)
    return pl.pallas_call(
        pack_kernel,
        out_shape=jax.ShapeDtypeStruct((heads, 3 * HEAD_DIM, tokens), BF16),
        in_specs=[hbm] * 3,
        out_specs=hbm,
        scratch_shapes=[
            pltpu.VMEM((3, tokens, width), BF16),
            pltpu.VMEM((heads, 3 * HEAD_DIM, tokens), BF16),
            pltpu.SemaphoreType.DMA((steps, 3)),
            pltpu.SemaphoreType.DMA((steps,)),
        ],
        compiler_params=params(56),
        cost_estimate=SMALL,
        name="pack",
    )(query, key, value)


Q_ROWS = 512
K_ROWS = 1024
DEPTH = 2 * HEAD_DIM + 16
V_ROWS = HEAD_DIM + 16


def attend_kernel(qkv_ref, out_ref, key_buf, value_buf):
    slabs = qkv_ref.shape[0]
    length = slabs * LANES
    per_block = Q_ROWS // LANES
    largest = jnp.zeros((1, LANES), F32)
    for slab in range(slabs):
        rows = slice(slab * LANES, (slab + 1) * LANES)
        keys = qkv_ref[slab, HEAD_DIM : 2 * HEAD_DIM, :]
        turned = keys.T
        key_buf[rows, 0:HEAD_DIM] = turned
        key_buf[rows, HEAD_DIM : 2 * HEAD_DIM] = turned
        wide = keys.astype(F32)
        largest = jnp.maximum(largest, jnp.sum(wide * wide, axis=0, keepdims=True))
        value_buf[0:HEAD_DIM, rows] = qkv_ref[slab, 2 * HEAD_DIM : 3 * HEAD_DIM, :]
    key_buf[:, 2 * HEAD_DIM : DEPTH] = jnp.ones((length, DEPTH - 2 * HEAD_DIM), BF16)
    value_buf[HEAD_DIM:V_ROWS, :] = jnp.ones((V_ROWS - HEAD_DIM, length), BF16)
    key_bound = jnp.max(largest, axis=1, keepdims=True)

    def load_queries(block):
        return jnp.concatenate(
            [qkv_ref[block * per_block + j, 0:HEAD_DIM, :] for j in range(per_block)], axis=1
        )

    def store(block, total):
        result = (total[0:HEAD_DIM] / total[HEAD_DIM : HEAD_DIM + 1]).astype(BF16)
        for j in range(per_block):
            out_ref[block * per_block + j] = result[:, j * LANES : (j + 1) * LANES]

    first_row = lax.broadcasted_iota(jnp.int32, (DEPTH - 2 * HEAD_DIM, Q_ROWS), 0) == 0

    def step(block, least):
        queries = load_queries(block).astype(F32)
        bound = SCORE_SCALE * jnp.sqrt(
            jnp.sum(queries * queries, axis=0, keepdims=True) * key_bound
        )
        scaled = queries * SCORE_SCALE
        high = scaled.astype(BF16)
        low = (scaled - high.astype(F32)).astype(BF16)
        shift = jnp.where(first_row, -bound, 0.0).astype(BF16)
        stacked = jnp.concatenate([high, low, shift], axis=0)
        total = jnp.zeros((V_ROWS, Q_ROWS), F32)
        for part in range(length // K_ROWS):
            span = slice(part * K_ROWS, (part + 1) * K_ROWS)
            scores = jnp.dot(key_buf[span, :], stacked, preferred_element_type=F32)
            weights = jnp.exp2(scores).astype(BF16)
            total = total + jnp.dot(value_buf[:, span], weights, preferred_element_type=F32)
        store(block, total)
        return jnp.minimum(least, total[HEAD_DIM : HEAD_DIM + 1])

    least = lax.fori_loop(0, length // Q_ROWS, step, jnp.full((1, Q_ROWS), 1.0, F32))

    @pl.when(jnp.min(least) < SMALLEST_SUM)
    def _():
        def careful(block, _):
            queries = load_queries(block)

            def inner(part, state):
                top, total = state
                begin = pl.multiple_of(part * K_ROWS, K_ROWS)
                keys = key_buf[pl.ds(begin, K_ROWS), 0:HEAD_DIM]
                scores = jnp.dot(keys, queries, preferred_element_type=F32)
                higher = jnp.maximum(top, jnp.max(scores, axis=0, keepdims=True))
                weights = jnp.exp2((scores - higher) * SCORE_SCALE).astype(BF16)
                fade = jnp.exp2((top - higher) * SCORE_SCALE)
                added = jnp.dot(
                    value_buf[:, pl.ds(begin, K_ROWS)], weights, preferred_element_type=F32
                )
                return higher, total * fade + added

            start = (jnp.full((1, Q_ROWS), -1e30, F32), jnp.zeros((V_ROWS, Q_ROWS), F32))
            _, total = lax.fori_loop(0, length // K_ROWS, inner, start)
            store(block, total)
            return 0

        lax.fori_loop(0, length // Q_ROWS, careful, 0)


def attend(qkv):
    slabs = qkv.shape[0]
    length = slabs * LANES
    return pl.pallas_call(
        attend_kernel,
        out_shape=jax.ShapeDtypeStruct((slabs, HEAD_DIM, LANES), BF16),
        in_specs=[vmem_spec()],
        out_specs=vmem_spec(),
        scratch_shapes=[pltpu.VMEM((length, DEPTH), BF16), pltpu.VMEM((V_ROWS, length), BF16)],
        compiler_params=params(20),
        cost_estimate=SMALL,
        name="attend",
    )(qkv)


def stage(sources, buffers, sems):
    copies = [
        pltpu.make_async_copy(source, buffer, sems.at[i])
        for i, (source, buffer) in enumerate(zip(sources, buffers))
    ]
    for copy in copies:
        copy.start()
    return copies


def hidden_kernel(pieces, y_ref, *refs):
    arrays = sum(count for _, count in pieces)
    clips = len(pieces)
    parts, refs = refs[:arrays], refs[arrays:]
    residual, out_hbm, first_hbm = refs[:3]
    near = () if clips > 1 else refs[3:4]
    refs = refs[3 + len(near) :]
    hidden_ref, *terms = refs[: 1 + clips]
    rows_buf, residual_buf, out_buf, first_buf, hidden_buf, sems = refs[1 + clips :]
    inner = out_buf.shape[0]
    chunks = 4
    depth = inner // chunks
    span = first_buf.shape[0] // 2
    sources = list(parts) + [residual]
    buffers = []
    for clip, (_, count) in enumerate(pieces):
        size = inner // count
        buffers += [rows_buf.at[clip, pl.ds(k * size, size)] for k in range(count)]
    buffers.append(residual_buf)
    for k in range(chunks):
        sources.append(out_hbm.at[pl.ds(k * depth, depth)])
        buffers.append(out_buf.at[pl.ds(k * depth, depth)])
    for k in range(2):
        sources.append(first_hbm.at[pl.ds(k * span, span)])
        buffers.append(first_buf.at[pl.ds(k * span, span)])
    if near:
        sources += [near[0].at[pl.ds(0, 2)], near[0].at[2]]
        buffers += [hidden_buf.at[pl.ds(0, 2)], hidden_buf.at[3]]
    copies = stage(sources, buffers, sems)
    for copy in copies[: arrays + 1]:
        copy.wait()
    tokens = rows_buf.shape[2]
    mixed = jnp.concatenate(
        [residual_buf[lax.rem(y_ref[0] + r, NY)].astype(F32) for r, _ in pieces], axis=0
    )
    for k in range(chunks):
        part = slice(k * depth, (k + 1) * depth)
        rows = jnp.concatenate([rows_buf[clip, part, :].T for clip in range(clips)], axis=0)
        copies[arrays + 1 + k].wait()
        mixed = mixed + jnp.dot(rows, out_buf[part, :], preferred_element_type=F32)
    hidden = mixed.astype(BF16)
    for clip in range(clips):
        hidden_buf[2 if near else clip] = hidden[clip * tokens : (clip + 1) * tokens]
    for copy in copies[arrays + 1 + chunks :]:
        copy.wait()
    last = pltpu.make_async_copy(hidden_buf, hidden_ref, sems.at[len(sources)])
    last.start()
    for clip, ref in enumerate(terms):
        rows = hidden[clip * tokens : (clip + 1) * tokens]
        ref[...] = jnp.dot(rows, first_buf[...], preferred_element_type=F32).astype(BF16)
    last.wait()


def hidden_rows(pieces, y, parts, residual, out_wide, first_wide, *near):
    inner = out_wide.shape[0]
    tokens = parts[0].shape[1]
    width, hid = first_wide.shape
    clips = len(pieces)
    return pl.pallas_call(
        functools.partial(hidden_kernel, pieces),
        out_shape=(
            jax.ShapeDtypeStruct((NY if near else clips, tokens, width), BF16),
            *[jax.ShapeDtypeStruct((tokens, hid), BF16)] * clips,
        ),
        in_specs=[pl.BlockSpec(memory_space=pltpu.SMEM)]
        + [pl.BlockSpec(memory_space=pl.ANY)] * (3 + len(parts) + len(near)),
        out_specs=(pl.BlockSpec(memory_space=pl.ANY), *[vmem_spec()] * clips),
        scratch_shapes=[
            pltpu.VMEM((clips, inner, tokens), BF16),
            pltpu.VMEM((NY, tokens, width), BF16),
            pltpu.VMEM((inner, width), BF16),
            pltpu.VMEM((width, hid), BF16),
            pltpu.VMEM((NY if near else clips, tokens, width), BF16),
            pltpu.SemaphoreType.DMA((len(parts) + 8 + 2 * len(near),)),
        ],
        compiler_params=params(56),
        cost_estimate=SMALL,
        name="hidden",
    )(y.reshape(1), *parts, residual, out_wide, first_wide, *near)


def similar_kernel(
    place_ref, own_hbm, one_hbm, two_hbm, three_hbm, target_hbm, own_0, own_1, own_3, own_2, own_2b,
    peer_0, peer_1, peer_3, peer_2, peer_2b, first_bias_ref, second_bias_ref, send_0, send_1, send_2, send_3, pre_grad_ref, cosine_ref,
    terms_ref, target_ref, second_ref, active_ref, slope_ref, sems,
):
    hid, outf = second_ref.shape
    depth = own_0.shape[0]
    sources = [own_hbm, one_hbm, two_hbm, three_hbm]
    buffers = [terms_ref.at[r] for r in range(NY)]
    spans = []
    for parity, second in (
        (place_ref[1], (own_0, own_1, own_3, own_2, own_2b)),
        (1 - place_ref[1], (peer_0, peer_1, peer_3, peer_2, peer_2b)),
    ):
        for piece, r in zip(second, (0, 1, 3, 2, 2)):
            rows = piece.shape[0]
            owner = 2 * lax.rem(place_ref[0] + r, NY) + parity
            begin = owner * depth + (rows if piece is second[-1] else 0)
            spans.append(pl.ds(pl.multiple_of(begin, rows), rows))
            sources.append(piece)
            buffers.append(second_ref.at[spans[-1]])
    copies = stage(sources + [target_hbm], buffers + [target_ref], sems)
    for copy in copies[:NY]:
        copy.wait()
    preact = first_bias_ref[...] + sum(terms_ref[r].astype(F32) for r in range(NY))
    gate = 1.0 / (1.0 + jnp.exp(-preact))
    active_ref[...] = (preact * gate).astype(BF16)
    slope_ref[...] = gate * (1.0 + preact * (1.0 - gate))
    projected = jnp.broadcast_to(second_bias_ref[...], target_ref.shape)
    for k, span in enumerate(spans):
        copies[NY + k].wait()
        projected = projected + jnp.dot(
            active_ref[:, span], second_ref[span, :], preferred_element_type=F32
        )
    copies[-1].wait()
    target = target_ref[...]
    inv_model = lax.rsqrt(jnp.sum(projected * projected, axis=1, keepdims=True) + EPSILON)
    inv_target = lax.rsqrt(jnp.sum(target * target, axis=1, keepdims=True) + EPSILON)
    cosine = jnp.sum(projected * target, axis=1, keepdims=True) * inv_model * inv_target
    cosine_ref[...] = cosine
    row_grad = (
        -math.sqrt(outf) * inv_model * (target * inv_target - cosine * inv_model * projected)
    ).astype(BF16)
    units = hid // NY
    for r, send in enumerate((send_0, send_1, send_2, send_3)):
        chip = lax.rem(place_ref[0] + (NY - r), NY)
        send[:, :units] = active_ref[:, pl.ds(pl.multiple_of(chip * units, units), units)]
        send[:, units:] = row_grad
    cols = hid // NX
    for quarter in range(NX):
        span = slice(quarter * cols, (quarter + 1) * cols)
        back = lax.dot_general(
            row_grad, second_ref[span, :], (((1,), (1,)), ((), ())), preferred_element_type=F32
        )
        pre_grad_ref[quarter] = (back * slope_ref[:, span]).astype(BF16)


def similar(place, terms, first_bias, seconds, second_bias, target):
    tokens, hid = terms[0].shape
    outf = seconds[0].shape[1]
    send = jax.ShapeDtypeStruct((tokens, hid // NY + outf), BF16)
    specs = [pl.BlockSpec(memory_space=pl.ANY)] * (NY + 1 + len(seconds)) + [vmem_spec()] * 2
    return pl.pallas_call(
        similar_kernel,
        out_shape=(
            (send,) * NY
            + (
                jax.ShapeDtypeStruct((NX, tokens, hid // NX), BF16),
                jax.ShapeDtypeStruct((tokens, 1), F32),
            )
        ),
        in_specs=[pl.BlockSpec(memory_space=pltpu.SMEM)] + specs,
        out_specs=(vmem_spec(),) * (NY + 2),
        scratch_shapes=[
            pltpu.VMEM((NY, tokens, hid), BF16),
            pltpu.VMEM((tokens, outf), F32),
            pltpu.VMEM((hid, outf), BF16),
            pltpu.VMEM((tokens, hid), BF16),
            pltpu.VMEM((tokens, hid), F32),
            pltpu.SemaphoreType.DMA((NY + 1 + len(seconds),)),
        ],
        compiler_params=params(56),
        cost_estimate=SMALL,
        name="similar",
    )(
        place, *terms, target, *seconds, first_bias.reshape(1, -1),
        second_bias.reshape(1, -1),
    )


def second_kernel(core_ref, one, two, three, four, keep_ref, give_ref):
    units = 2 * keep_ref.shape[1]
    cols = keep_ref.shape[2]
    parts = (one, two, three, four)
    active = jnp.concatenate([part[:, :units] for part in parts], axis=0).T
    grads = [
        jnp.concatenate(
            [part[:, units + x * cols : units + (x + 1) * cols] for part in parts], axis=0
        )
        for x in range(NX)
    ]
    half = units // 2
    for x in range(NX):
        total = jnp.dot(active, grads[x], preferred_element_type=F32).astype(BF16)
        top, bottom = total[:half], total[half:]
        first = core_ref[0] == 0
        keep_ref[x] = jnp.where(first, top, bottom)
        give_ref[x] = jnp.where(first, bottom, top)


def second_gradient(core, parts, units, outf):
    shape = jax.ShapeDtypeStruct((NX, units, outf // NX), BF16)
    return pl.pallas_call(
        second_kernel,
        out_shape=(shape, shape),
        in_specs=[pl.BlockSpec(memory_space=pltpu.SMEM)] + [vmem_spec()] * NY,
        out_specs=(vmem_spec(), vmem_spec()),
        compiler_params=params(24),
        cost_estimate=LARGE,
        name="second",
    )(core.reshape(1), *parts)


def first_kernel(clips, x_ref, *refs):
    hidden_own, hidden_up, hidden_down, hidden_top, hidden_bottom = refs[:5]
    refs = refs[5:]
    arrays = sum(count for _, count in clips)
    parts, refs = refs[:arrays], refs[arrays:]
    last = len(clips) == 1
    if last:
        before, keep_ref, give_ref, hidden_buf, grad_buf, total_buf, sems = refs
    else:
        total_ref, hidden_buf, grad_buf, sems = refs
    sources = []
    buffers = []
    half = NY // 2
    for i, (r, count) in enumerate(clips):
        across = hidden_top.at[r] if r < half else hidden_bottom.at[r - half]
        for d, source in enumerate((hidden_own.at[r], hidden_up.at[r], across, hidden_down.at[r])):
            sources.append(source)
            buffers.append(hidden_buf.at[i, lax.rem(x_ref[0] + d, NX)])
        size = NX // count
        buffers += [grad_buf.at[i, pl.ds(k * size, size)] for k in range(count)]
        sources += parts[:count]
        parts = parts[count:]
    if last:
        sources.append(before)
        buffers.append(total_buf)
    copies = stage(sources, buffers, sems)
    total = 0.0
    for i, (_, count) in enumerate(clips):
        for copy in copies[: count + NX]:
            copy.wait()
        copies = copies[count + NX :]
        left = hidden_buf[i].reshape(-1, hidden_buf.shape[3])
        right = grad_buf[i].reshape(-1, grad_buf.shape[3])
        total = total + jnp.dot(left.T, right, preferred_element_type=F32)
    if last:
        width = keep_ref.shape[0]
        copies[0].wait()
        total = total + total_buf[...]
        keep_ref[...] = total[:width].astype(BF16)
        give_ref[...] = total[width:].astype(BF16)
    else:
        total_ref[...] = total


def first_gradient(clips, x, hidden, grads, *before):
    _, tokens, width = hidden[0].shape
    cols = grads[0].shape[2]
    if before:
        out_shape = (jax.ShapeDtypeStruct((width // 2, cols), BF16),) * 2
    else:
        out_shape = jax.ShapeDtypeStruct((width, cols), F32)
    return pl.pallas_call(
        functools.partial(first_kernel, clips),
        out_shape=out_shape,
        in_specs=[pl.BlockSpec(memory_space=pltpu.SMEM)]
        + [pl.BlockSpec(memory_space=pl.ANY)] * (len(hidden) + len(grads) + len(before)),
        out_specs=(vmem_spec(), vmem_spec()) if before else vmem_spec(),
        scratch_shapes=[
            pltpu.VMEM((len(clips), NX, tokens, width), BF16),
            pltpu.VMEM((len(clips), NX, tokens, cols), BF16),
            *[pltpu.VMEM(total.shape, F32) for total in before],
            pltpu.SemaphoreType.DMA((NX * len(clips) + len(grads) + len(before),)),
        ],
        compiler_params=params(56),
        cost_estimate=SMALL,
        name="first",
    )(x.reshape(1), *hidden, *grads, *before)


def arrange_kernel(pair_ref, own_ref, other_ref, second_ref, *refs):
    *outs, first_sum, second_sum = refs
    first_sum[...] = (own_ref[...].astype(F32) + other_ref[...].astype(F32)).astype(BF16)
    second = second_ref[0].astype(F32)
    for x in range(1, NX):
        second = second + second_ref[x].astype(F32)
    second_sum[...] = second.astype(BF16)
    for step, out_ref in enumerate(outs):
        pair = lax.rem(pair_ref[0] + step, NZ // 2)
        for parity in range(2):
            row = 0
            for total in (first_sum, second_sum):
                rows = total.shape[0] // NZ
                begin = pl.multiple_of((2 * pair + parity) * rows, rows)
                for lane in range(total.shape[1] // LANES):
                    out_ref[parity, row : row + rows, :] = total[
                        pl.ds(begin, rows), lane * LANES : (lane + 1) * LANES
                    ]
                    row += rows


def arrange(pair, own, other, second):
    rows = (own.size + second[0].size) // (NZ * LANES)
    return pl.pallas_call(
        arrange_kernel,
        out_shape=(jax.ShapeDtypeStruct((2, rows, LANES), BF16),) * (NZ // 2),
        in_specs=[pl.BlockSpec(memory_space=pltpu.SMEM)] + [vmem_spec()] * 3,
        out_specs=(vmem_spec(),) * (NZ // 2),
        scratch_shapes=[pltpu.VMEM(own.shape, BF16), pltpu.VMEM(second.shape[1:], BF16)],
        compiler_params=params(16),
        cost_estimate=SMALL,
        name="arrange",
    )(pair.reshape(1), own, other, second)


def part_kernel(parity_ref, *refs):
    *blocks, keep_ref, give_ref = refs
    for index, ref in ((parity_ref[0], keep_ref), (1 - parity_ref[0], give_ref)):
        ref[...] = sum(block[index].astype(F32) for block in blocks).astype(ref.dtype)


def part(parity, blocks):
    shape = blocks[0].shape[1:]
    return pl.pallas_call(
        part_kernel,
        out_shape=(jax.ShapeDtypeStruct(shape, F32), jax.ShapeDtypeStruct(shape, BF16)),
        in_specs=[pl.BlockSpec(memory_space=pltpu.SMEM)] + [vmem_spec()] * len(blocks),
        out_specs=(vmem_spec(), vmem_spec()),
        compiler_params=params(16),
        cost_estimate=SMALL,
        name="part",
    )(parity.reshape(1), *blocks)


def unpack_kernel(place_ref, *refs):
    *parts, first_ref, second_ref = refs
    for index, part in enumerate(parts):
        column = lax.rem(place_ref[0] + index // 2, NX)
        parity = lax.rem(place_ref[1] + index % 2, 2)
        for pair in range(NZ // 2):
            z = 2 * lax.rem(place_ref[1] // 2 + pair, NZ // 2) + parity
            row = 0
            for ref in (first_ref, second_ref):
                rows = ref.shape[0] // NZ
                cols = ref.shape[1] // NX
                to_row = pl.multiple_of(z * rows, rows)
                for lane in range(cols // LANES):
                    to_lane = pl.multiple_of(column * cols + lane * LANES, LANES)
                    ref[pl.ds(to_row, rows), pl.ds(to_lane, LANES)] = part[
                        pair, row : row + rows, :
                    ]
                    row += rows


def unpack(place, parts, first_shape, second_shape):
    return pl.pallas_call(
        unpack_kernel,
        out_shape=(
            jax.ShapeDtypeStruct(first_shape, BF16),
            jax.ShapeDtypeStruct(second_shape, BF16),
        ),
        in_specs=[pl.BlockSpec(memory_space=pltpu.SMEM)] + [vmem_spec()] * len(parts),
        out_specs=(vmem_spec(), vmem_spec()),
        compiler_params=params(16),
        cost_estimate=SMALL,
        name="unpack",
    )(place, *parts)


def after(values, *others):
    return lax.optimization_barrier((values, others))[0]


def body(
    query_in,
    key_in,
    value_in,
    residual,
    out_proj,
    first_proj,
    first_bias,
    second_proj,
    second_bias,
    teacher,
    teach_index,
    teach_weight,
):
    dp = lax.axis_index("dp")
    seq = lax.axis_index("seq")
    y, core = dp // 2, lax.rem(dp, 2)
    x = seq // NZ
    tokens = query_in.shape[1]
    width = residual.shape[2]
    hid = first_bias.shape[0]
    outf = second_bias.shape[0]

    swap = functools.partial(lax.ppermute, axis_name="dp", perm=core_swap())

    def from_y(value, by):
        return lax.ppermute(value, "dp", dp_shift(-by))

    seconds = [second_proj, from_y(second_proj, 1), from_y(second_proj, 3)]
    middle = second_proj.shape[0] // 2
    seconds += [from_y(seconds[1][:middle], 1), from_y(seconds[2][middle:], 3)]
    peers = [swap(second_proj)]
    out_wide = jnp.concatenate([out_proj, swap(out_proj)], axis=1)
    first_wide = jnp.concatenate([first_proj, swap(first_proj)], axis=0)
    by_core = residual.reshape(NY, 2, tokens, width)
    mine = lax.dynamic_index_in_dim(by_core, core, 1, keepdims=False)
    theirs = lax.dynamic_index_in_dim(by_core, 1 - core, 1, keepdims=False)
    residual_wide = jnp.concatenate([mine, swap(theirs)], axis=2)

    local = teacher[0]
    rows = local.shape[0]
    count = lax.axis_size("seq")
    earlier = lax.ppermute(local, "seq", [(i, i + 1) for i in range(count - 1)])
    later = lax.ppermute(local, "seq", [(i + 1, i) for i in range(count - 1)])
    window = jnp.concatenate([earlier, local, later], axis=0)
    offsets = teach_index - (seq - 1) * rows
    spots = jnp.arange(3 * rows, dtype=jnp.int32)
    blend = jnp.sum(
        jnp.where(offsets[:, :, None] == spots, teach_weight[:, :, None], 0.0), axis=1
    )

    qkv = lax.all_to_all(
        pack(query_in[0], key_in[0], value_in[0]), "seq", 0, 0, tiled=True
    )
    qkv = after(qkv, out_wide, first_wide, residual_wide, seconds, peers[0])
    attended = lax.all_to_all(attend(qkv), "seq", 0, 0, tiled=True)
    peers += [swap(second) for second in seconds[1:]]
    attended = after(attended.reshape(-1, tokens), peers)

    def from_x(value, by):
        return lax.ppermute(value, "seq", x_shift(-by))

    half = attended.shape[0] // 2
    upper = from_y(attended, 1)
    lower = from_y(attended, 3)
    across = [from_y(upper[:half], 1), from_y(lower[half:], 3)]
    (upper, lower), window = lax.optimization_barrier(((upper, lower), window))
    target = jnp.dot(blend, window.astype(F32), precision=lax.Precision.HIGHEST)
    near, *near_terms = hidden_rows(
        ((0, 1), (1, 1), (3, 1)), y, [attended, upper, lower], residual_wide, out_wide, first_wide
    )
    across = after(across, near)
    hidden, far_term = hidden_rows(
        ((2, 2),), y, across, residual_wide, out_wide, first_wide, near
    )
    terms = [
        near_terms[0],
        lax.ppermute(near_terms[1], "dp", dp_shift(1)),
        lax.ppermute(far_term, "dp", dp_shift(2)),
        lax.ppermute(near_terms[2], "dp", dp_shift(3)),
    ]

    hidden_up = from_x(hidden, 1)
    hidden_down = from_x(hidden, 3)
    terms = after(terms, hidden_up, hidden_down)
    hidden_x = [
        hidden,
        hidden_up,
        hidden_down,
        from_x(hidden_up[: NY // 2], 1),
        from_x(hidden_down[NY // 2 :], 3),
    ]

    *sends, pre_grad, cosine = similar(
        jnp.stack([y, core]), terms, first_bias, seconds + peers, second_bias, target
    )
    pre_grad = after(pre_grad, hidden_x)
    sends = [sends[0]] + [from_y(sends[r], r) for r in range(1, NY)]

    pre_x = lax.all_to_all(pre_grad, "seq", 0, 0, tiled=True, axis_index_groups=X_GROUPS)
    upper = from_y(pre_x, 1)
    lower = from_y(pre_x, 3)

    units = second_proj.shape[0]
    keep, give = second_gradient(core, after(sends, pre_x), units, outf)
    second_own = (keep.astype(F32) + swap(give).astype(F32)).astype(BF16)
    upper, lower = after((upper, lower), second_own)
    across = [from_y(upper[: NX // 2], 1), from_y(lower[NX // 2 :], 3)]
    second_parts = lax.all_to_all(
        second_own, "seq", 0, 0, tiled=True, axis_index_groups=X_GROUPS
    )
    total = first_gradient(((1, 1), (3, 1), (0, 1)), x, hidden_x, [upper, lower, pre_x])
    across = after(across, total)
    first_own, first_give = first_gradient(((2, 2),), x, hidden_x, across, total)

    z = lax.rem(seq, NZ)
    blocks = arrange(z // 2, first_own, swap(first_give), second_parts)

    def from_pair(value, by):
        return lax.ppermute(value, "seq", pair_shift(-by))

    blocks = [blocks[0]] + [from_pair(blocks[k], -k) for k in (1, 3, 2)]
    keep, give = part(lax.rem(z, 2), blocks)
    summed = (keep + lax.ppermute(give, "seq", z_swap()).astype(F32)).astype(BF16)

    same = jnp.stack([summed] + [from_pair(summed, k) for k in range(1, NZ // 2)])
    other = lax.ppermute(same, "seq", z_swap())
    same_x = {0: same, 1: from_x(same, 1), 3: from_x(same, 3)}
    other_x = {0: other, 1: from_x(other, 1), 3: from_x(other, 3)}
    same_x[2] = from_x(same_x[1], 1)
    other_x[2] = from_x(other_x[3], 3)
    grad_first, grad_second = unpack(
        jnp.stack([x, z]),
        [part for d in range(NX) for part in (same_x[d], other_x[d])],
        (width, hid),
        (units, outf),
    )
    return (cosine.reshape(1, -1), grad_first, grad_second)


def solution(mesh):
    placed = (
        P("dp", "seq", None),
        P("dp", "seq", None),
        P("dp", "seq", None),
        P(None, "seq", "dp"),
        P(None, "dp"),
        P("dp", None),
        P(),
        P("dp", None),
        P(),
        P("dp", "seq", None),
        P("seq", None),
        P("seq", None),
    )
    return jax.shard_map(
        body,
        mesh=mesh,
        in_specs=placed,
        out_specs=(P("dp", "seq"), P("dp", None), P("dp", None)),
        check_vma=False,
    )
```
